512 devices in a mesh: grp: 16 (over y, x), sub: 32 (over z, core).
Axes of the slice: x: 4, y: 4, z: 16, core: 2. Of those that a mesh axis runs over, the one named last changes fastest.
Arguments:
- right_side: float32 [393216, 160], P(('grp', 'sub')), may hold values from -6 to 6
- iterate_in: float32 [393216, 160], P(('grp', 'sub')), may hold values from -6 to 6
- diagonal: float32 [393216], P(('grp', 'sub')), may hold values from 1.5 to 4
- block_values: bfloat16 [512, 6, 3, 128, 128], P(('grp', 'sub')), may hold values from -0.125 to 0.125
- block_cols: int32 [512, 6, 3], P(('grp', 'sub')), may hold values from 0 to 5, as said below
- couple_left: bfloat16 [393216, 128], P(('grp', 'sub')), may hold values from -0.125 to 0.125
- couple_right: bfloat16 [393216, 128], P(('grp', 'sub')), may hold values from -0.125 to 0.125
- send_rows: int32 [512, 2, 128], P(('grp', 'sub')), may hold values from 0 to 767, as said below
- local_inverse: bfloat16 [512, 1024, 1024], P(('grp', 'sub')), may hold values from -0.3 to 2.3, as said below
- coarse_basis: bfloat16 [512, 1024, 32], P(('grp', 'sub')), may hold values from -0.1875 to 0.1875
- coarse_diag: float32 [512, 32, 32], P(('grp', 'sub')), may hold values from -54 to 59.5, as said below
- coarse_up: float32 [512, 32, 32], P(('grp', 'sub')), may hold values from -29.7 to 27
Outputs:
- iterate: float32 [393216, 160], P(('grp', 'sub'))
- residual: float32 [393216, 160], P(('grp', 'sub'))
The draws below stay inside these ranges and needn't reach their ends.
Inputs may be any that keep to these rules, and one draw needn't show every extreme that they name: `block_cols`: the 3 column blocks of one row block are distinct. `send_rows`: the 256 rows listed for one subdomain are distinct. `local_inverse`: each block is symmetric positive definite. `coarse_diag`: each block is symmetric; with coarse_up the coarse operator is symmetric positive definite.
All inputs are finite; a program needn't handle non-finite values.
Results may differ from the reference program's by a relative error of at most 0.0032.
Values may be sent and summed in bfloat16 or wider, within the bound.
A program may use at most 64 MiB of HBM per device.

```python
import math
import jax
import jax.numpy as jnp
from jax import lax

ROWS = 768
CASES = 160
INTERSECTION = 128
BLOCK = 128
NONZEROS = 3
MODES = 32
ROW_BLOCKS = 6
EXTENDED = 1024
SUBDOMAINS = 512
UNKNOWNS = 393216


def draw_block_cols(key, part):
    keys = jax.random.split(jax.random.fold_in(key, 3), SUBDOMAINS * ROW_BLOCKS)

    def one_row(row_key):
        return jax.random.permutation(row_key, ROW_BLOCKS)[:NONZEROS]
    return jax.vmap(one_row)(keys).reshape(SUBDOMAINS, ROW_BLOCKS, NONZEROS).astype(jnp.int32)


def draw_send_rows(key, part):
    keys = jax.random.split(jax.random.fold_in(key, 5), SUBDOMAINS)

    def one_domain(domain_key):
        return jax.random.permutation(domain_key, ROWS)[:2 * INTERSECTION]
    return jax.vmap(one_domain)(keys).reshape(SUBDOMAINS, 2, INTERSECTION).astype(jnp.int32)


def draw_local_inverse(key, part):
    noise_key, diag_key = jax.random.split(jax.random.fold_in(key, 7))
    noise = jnp.clip(jax.random.normal(noise_key, (SUBDOMAINS, EXTENDED, EXTENDED), jnp.float32), -4.0, 4.0) * (0.25 / math.sqrt(EXTENDED))
    symmetric = noise + jnp.swapaxes(noise, 1, 2)
    low_end = 1.0
    diag_values = jax.random.uniform(diag_key, (SUBDOMAINS, EXTENDED, 1), jnp.float32, low_end, 2.0)
    return (symmetric + diag_values * jnp.eye(EXTENDED, dtype=jnp.float32)).astype(jnp.bfloat16)


def edge_couplings(key):
    strength_key, factor_key = jax.random.split(jax.random.fold_in(key, 11))
    root_three = math.sqrt(3.0)
    factor = jax.random.uniform(factor_key, (SUBDOMAINS, MODES, MODES), jnp.float32, -root_three, root_three)
    product = jnp.einsum('kab,kcb->kac', factor, factor, precision=jax.lax.Precision.HIGHEST) / MODES
    product = 0.5 * (product + jnp.swapaxes(product, 1, 2))
    strength = jnp.exp(jax.random.uniform(strength_key, (SUBDOMAINS, 1, 1), jnp.float32, math.log(3.0), math.log(9.0)))
    return strength * (0.3 * jnp.eye(MODES, dtype=jnp.float32) + product)


def draw_coarse_diag(key, part):
    coupling = edge_couplings(key)
    shift_key = jax.random.fold_in(key, 17)
    shift_low = 0.005
    shift_high = 0.02
    shifts = jnp.exp(jax.random.uniform(shift_key, (SUBDOMAINS, MODES, 1), jnp.float32, math.log(shift_low), math.log(shift_high)))
    inside = (jnp.arange(SUBDOMAINS) < SUBDOMAINS - 1).astype(jnp.float32)[:, None, None]
    own = coupling * inside
    previous = jnp.concatenate([jnp.zeros_like(coupling[:1]), own[:-1]], axis=0)
    return own + previous + shifts * jnp.eye(MODES, dtype=jnp.float32)


def draw_coarse_up(key, part):
    return -edge_couplings(key)


def levels(rng, extent, pieces, least, high):
    def one(dim, parts):
        heights = jax.random.uniform(jax.random.fold_in(jax.random.fold_in(rng, 6), dim), (parts,), jnp.float32, least / len(pieces), high / len(pieces))
        return jnp.repeat(jnp.exp(heights), extent[dim] // parts).reshape((-1,) + (1,) * (len(extent) - dim - 1))

    factor_of = one(*pieces[0])
    for cut in pieces[1:]:
        factor_of = factor_of * one(*cut)
    return factor_of


def centred(key, extent, deviation, limit, pieces=(), kind=jnp.bfloat16):
    entries = deviation * jax.random.normal(key, extent, jnp.float32)
    if pieces:
        entries = entries * levels(key, extent, pieces, -0.22, 0.18)
    return jnp.clip(entries, -limit, limit).astype(kind)


def setup_inputs(seed: int = 0) -> dict:
    splits = jax.random.split(jax.random.key(seed), 13)
    return {
        "right_side": centred(splits[0], (UNKNOWNS, CASES), 1.0, 6.0, ((0, 512),), jnp.float32),
        "iterate_in": centred(splits[1], (UNKNOWNS, CASES), 1.0, 6.0, ((0, 512),), jnp.float32),
        "diagonal": jnp.clip(jnp.exp(math.log(4.0) - 0.98082925 * jax.random.uniform(splits[2], (UNKNOWNS,), jnp.float32) ** levels(splits[2], (UNKNOWNS,), ((0, 512),), -0.2, 0.2)), 1.5, 4.0),
        "block_values": centred(splits[3], (SUBDOMAINS, ROW_BLOCKS, NONZEROS, BLOCK, BLOCK), (4 * (NONZEROS * BLOCK + 2 * INTERSECTION)) ** -0.5, 0.125, ((0, 512),)),
        "block_cols": draw_block_cols(jax.random.fold_in(splits[12], 71), 0),
        "couple_left": centred(splits[5], (UNKNOWNS, INTERSECTION), (4 * (NONZEROS * BLOCK + 2 * INTERSECTION)) ** -0.5, 0.125, ((0, 512),)),
        "couple_right": centred(splits[6], (UNKNOWNS, INTERSECTION), (4 * (NONZEROS * BLOCK + 2 * INTERSECTION)) ** -0.5, 0.125, ((0, 512),)),
        "send_rows": draw_send_rows(jax.random.fold_in(splits[12], 71), 0),
        "local_inverse": draw_local_inverse(jax.random.fold_in(splits[12], 71), 0),
        "coarse_basis": centred(splits[9], (SUBDOMAINS, EXTENDED, MODES), EXTENDED ** -0.5, 0.1875, ((0, 512),)),
        "coarse_diag": draw_coarse_diag(jax.random.fold_in(splits[12], 71), 0),
        "coarse_up": draw_coarse_up(jax.random.fold_in(splits[12], 71), 0),
    }


def chol_solve(factor, values):
    halfway = lax.linalg.triangular_solve(factor, values, left_side=True, lower=True)
    return lax.linalg.triangular_solve(factor, halfway, left_side=True, lower=True, transpose_a=True)

def solve_chain(diagonal_blocks, upper, values):
    highest = lax.Precision.HIGHEST
    width_up = upper.shape[2]
    first = jnp.linalg.cholesky(diagonal_blocks[0])

    def forward(state, entry):
        factor, reduced, coupling = state
        block_diag, block_up, block_rhs = entry
        through = chol_solve(factor, jnp.concatenate([coupling, reduced], axis=1))
        schur = block_diag - jnp.dot(coupling.T, through[:, :width_up], precision=highest)
        carried = block_rhs - jnp.dot(coupling.T, through[:, width_up:], precision=highest)
        new_factor = jnp.linalg.cholesky(schur)
        return ((new_factor, carried, block_up), (new_factor, carried))
    _, (factors, carried_all) = lax.scan(forward, (first, values[0], upper[0]), (diagonal_blocks[1:], upper[1:], values[1:]))
    factors = jnp.concatenate([first[None], factors], axis=0)
    carried_all = jnp.concatenate([values[0][None], carried_all], axis=0)
    final = chol_solve(factors[-1], carried_all[-1])

    def backward(later, entry):
        factor, reduced, coupling = entry
        current = chol_solve(factor, reduced - jnp.dot(coupling, later, precision=highest))
        return (current, current)
    _, earlier = lax.scan(backward, final, (factors[:-1], carried_all[:-1], upper[:-1]), reverse=True)
    return jnp.concatenate([earlier, final[None]], axis=0)

def pick_rows(values, indices):

    def chosen(source, index):
        return source[index]
    return jax.vmap(chosen)(values, indices)

def add_rows(values, indices, addend):

    def placed(source, index, extra):
        return source.at[index].add(extra)
    return jax.vmap(placed)(values, indices, addend)

def reference(right_side, iterate_in, diagonal, block_values, block_cols, couple_left, couple_right, send_rows, local_inverse, coarse_basis, coarse_diag, coarse_up):
    bf16 = jnp.bfloat16
    f32 = jnp.float32
    left_all = couple_left.reshape(SUBDOMAINS, ROWS, INTERSECTION)
    right_all = couple_right.reshape(SUBDOMAINS, ROWS, INTERSECTION)
    diag_all = diagonal.reshape(SUBDOMAINS, ROWS, 1)

    def neighbours(rounded):
        sent_right = pick_rows(rounded, send_rows[:, 1])
        sent_left = pick_rows(rounded, send_rows[:, 0])
        nothing = jnp.zeros_like(sent_right[:1])
        from_left = jnp.concatenate([nothing, sent_right[:-1]], axis=0)
        from_right = jnp.concatenate([sent_left[1:], nothing], axis=0)
        return (from_left, from_right)

    def apply_operator(vector):
        rounded = vector.astype(bf16)
        from_left, from_right = neighbours(rounded)

        def one_domain(entry):
            values_here, cols_here, rows_here, left_here, right_here, left_coupling, right_coupling = entry
            blocks = rows_here.reshape(ROW_BLOCKS, BLOCK, CASES)
            picked = blocks[cols_here]
            sparse = jnp.einsum('itab,itbn->ian', values_here.astype(f32), picked.astype(f32)).reshape(ROWS, CASES)
            coupled = jnp.dot(left_coupling, left_here, preferred_element_type=f32) + jnp.dot(right_coupling, right_here, preferred_element_type=f32)
            return sparse + coupled
        offdiag = lax.map(one_domain, (block_values, block_cols, rounded, from_left, from_right, left_all, right_all))
        return diag_all * vector + offdiag

    def precondition(residual_in):
        rounded = residual_in.astype(bf16)
        from_left, from_right = neighbours(rounded)
        extended = jnp.concatenate([from_left, rounded, from_right], axis=1)

        def local_step(entry):
            inverse, basis, margin = entry
            return (jnp.dot(inverse, margin, preferred_element_type=f32), jnp.dot(basis.T, margin, preferred_element_type=f32))
        local_part, coarse_in = lax.map(local_step, (local_inverse, coarse_basis, extended))
        coarse_sol = solve_chain(coarse_diag, coarse_up, coarse_in)

        def lift(entry):
            basis, solution = entry
            return jnp.dot(basis, solution.astype(bf16), preferred_element_type=f32)
        correction = local_part + lax.map(lift, (coarse_basis, coarse_sol))
        owned = correction[:, INTERSECTION:INTERSECTION + ROWS]
        nothing = jnp.zeros_like(correction[:1, :INTERSECTION])
        from_next = jnp.concatenate([correction[1:, :INTERSECTION], nothing], axis=0)
        from_prev = jnp.concatenate([nothing, correction[:-1, INTERSECTION + ROWS:]], axis=0)
        owned = add_rows(owned, send_rows[:, 1], from_next)
        owned = add_rows(owned, send_rows[:, 0], from_prev)
        return owned
    loads = right_side.reshape(SUBDOMAINS, ROWS, CASES)
    start = iterate_in.reshape(SUBDOMAINS, ROWS, CASES)
    residual_start = loads - apply_operator(start)
    precond = precondition(residual_start)
    inner = jnp.sum(residual_start * precond, axis=(0, 1))
    image = apply_operator(precond)
    curvature = jnp.sum(precond * image, axis=(0, 1))
    step_size = inner / curvature
    iterate = start + step_size * precond
    residual = residual_start - step_size * image
    return (iterate.reshape(UNKNOWNS, CASES), residual.reshape(UNKNOWNS, CASES))
```

```python
import functools

import jax
import jax.numpy as jnp
from jax import lax
from jax.experimental import pallas as pl
from jax.experimental.pallas import tpu as pltpu
from jax.sharding import PartitionSpec as P

MESH = pl.DeviceIdType.MESH
HIGHEST = lax.Precision.HIGHEST
F32 = jnp.float32
BF16 = jnp.bfloat16
SEG = 8
SLICE = 3


def dot(a, b, ca=1, cb=0, precision=None):
    return lax.dot_general(
        a, b, (((ca,), (cb,)), ((), ())), precision=precision, preferred_element_type=F32
    )


def pack_block(x):
    return jnp.concatenate([x[8 * i : 8 * i + 8] for i in range(4)], axis=1)


def unpack_block(t):
    return jnp.concatenate([t[:, 32 * i : 32 * i + 32] for i in range(4)], axis=0)


def pack_slice(x):
    zeros = jnp.zeros((8, 32), F32)
    return jnp.concatenate([x[8 * i : 8 * i + 8] for i in range(SLICE)] + [zeros], axis=1)


def unpack_slice(t):
    return jnp.concatenate([t[:, 32 * i : 32 * i + 32] for i in range(SLICE)], axis=0)


def gauss_jordan(mats):
    count = len(mats)
    below = lax.broadcasted_iota(jnp.int32, (8, 128), 0)

    def eight(_, flat):
        groups = [list(flat[4 * m : 4 * m + 4]) for m in range(count)]
        for p in range(8):
            for g in groups:
                row = g[0][p : p + 1, :]
                scaled = row * (1.0 / row[:, p : p + 1])
                updated = [g[i] - g[i][:, p : p + 1] * scaled for i in range(4)]
                updated[0] = jnp.where(below == p, jnp.broadcast_to(scaled, (8, 128)), updated[0])
                g[:] = updated
        out = []
        for g in groups:
            out += [pltpu.roll(g[i], 120, 1) for i in (1, 2, 3, 0)]
        return tuple(out)

    flat = tuple(m[8 * i : 8 * i + 8] for m in mats for i in range(4))
    flat = lax.fori_loop(0, 4, eight, flat)
    return [jnp.concatenate(flat[4 * m : 4 * m + 4], axis=0) for m in range(count)]


def levels_of(n):
    nodes = list(range(n))
    levels = []
    while len(nodes) > 1:
        ends = nodes + [n]
        levels.append([(ends[q], ends[q - 1], ends[q + 1]) for q in range(1, len(nodes), 2)])
        nodes = nodes[0::2]
    return levels


def identity_block():
    return (
        lax.broadcasted_iota(jnp.int32, (32, 32), 0) == lax.broadcasted_iota(jnp.int32, (32, 32), 1)
    ).astype(F32)


def eliminate(n, diag, up, low, factors):
    diag, up, low = list(diag), list(up), list(low)
    eye = identity_block()
    for level in levels_of(n):
        augmented = [
            jnp.concatenate([diag[o], low[e], up[o], eye], axis=1) for o, e, _ in level
        ]
        solved = gauss_jordan(augmented)
        for (o, e, f), before, after in zip(level, augmented, solved):
            factors[o] = after
            schur = dot(before, after, 0, 0, HIGHEST)
            diag[e] = diag[e] - schur[32:64, 0:32]
            diag[f] = diag[f] - schur[64:96, 32:64]
            up[e] = -schur[32:64, 32:64]
            low[e] = -schur[64:96, 0:32]
    return diag[0], up[0], low[0], diag[n]


def sweep_up(n, loads, factors):
    loads = list(loads)
    for level in levels_of(n):
        for o, e, f in level:
            moved = dot(loads[o], factors[o], 1, 0, HIGHEST)
            loads[e] = loads[e] - moved[:, 0:32]
            loads[f] = loads[f] - moved[:, 32:64]
    return loads


def sweep_down(n, loads, first, last, factors):
    sol = [None] * (n + 1)
    sol[0], sol[n] = first, last
    blank = jnp.zeros_like(first)
    for level in reversed(levels_of(n)):
        for o, e, f in level:
            known = jnp.concatenate([-sol[e], -sol[f], loads[o], blank], axis=1)
            sol[o] = dot(known, factors[o], 1, 1, HIGHEST)
    return sol


def kernel(
    n2,
    n3,
    cols_ref,
    rhs_hbm,
    start_hbm,
    diag_hbm,
    values_hbm,
    left_hbm,
    right_hbm,
    rows_hbm,
    inverse_hbm,
    basis_hbm,
    cdiag_hbm,
    cup_hbm,
    out_iterate,
    out_residual,
    rhs,
    start,
    diag_rows,
    diag_cols,
    values,
    dense,
    couple_left,
    couple_right,
    rows_v,
    inverse,
    basis,
    cdiag,
    cup,
    rounded,
    pick,
    spread,
    halo_out,
    halo_in,
    edge_out,
    edge_in,
    residual,
    extended,
    correction,
    owned,
    image,
    m1,
    m2,
    m3,
    s1_out,
    s1,
    s2,
    s3,
    s4_out,
    s4,
    f1,
    f2,
    f3,
    x2,
    x3,
    r1,
    r2,
    r3,
    load_sem,
    ring_send,
    ring_recv,
    seg_send,
    seg_recv,
    mid_send,
    mid_recv,
    top_send,
    top_recv,
):
    rows_own, cases = start.shape
    margin = rows_v.shape[1]
    row_blocks = diag_rows.shape[0]
    grp, sub = lax.axis_index("grp"), lax.axis_index("sub")
    members = n2 * SEG
    pos1, pos2 = lax.rem(sub, SEG), lax.div(sub, SEG)
    rank = grp * members + sub
    total = n3 * members
    sub_next, sub_prev = lax.rem(sub + 1, members), lax.rem(sub + members - 1, members)
    grp_next = lax.rem(grp + (sub + 1) // members, n3)
    grp_prev = lax.rem(grp + n3 - (members - sub) // members, n3)
    ring = [(grp_prev, sub_prev), (grp_next, sub_next)]
    has_prev, has_next = rank > 0, rank < total - 1

    def seg_other(off):
        j = lax.rem(pos1 + off, SEG)
        return j, (grp, pos2 * SEG + j)

    def mid_other(off):
        j = lax.rem(pos2 + off, n2)
        return j, (grp, j * SEG + pos1)

    def top_other(off):
        j = lax.rem(grp + off, n3)
        return j, (j, sub)

    kinds = {
        "seg": (SEG, pos1, seg_other, seg_send, seg_recv),
        "mid": (n2, pos2, mid_other, mid_send, mid_recv),
        "top": (n3, grp, top_other, top_send, top_recv),
    }

    loads = {}
    for name, source, target in (
        ("rows", rows_hbm.at[0], rows_v),
        ("start", start_hbm, start),
        ("cdiag", cdiag_hbm.at[0], cdiag),
        ("cup", cup_hbm.at[0], cup),
        ("diag", diag_hbm, diag_rows),
        ("values", values_hbm.at[0], values),
        ("left", left_hbm, couple_left),
        ("right", right_hbm, couple_right),
        ("rhs", rhs_hbm, rhs),
        ("basis", basis_hbm.at[0], basis),
        ("inverse", inverse_hbm.at[0], inverse),
    ):
        copy = pltpu.make_async_copy(source, target, load_sem.at[len(loads)])
        copy.start()
        loads[name] = copy

    barrier = pltpu.get_barrier_semaphore()
    greeted = 0
    for target in ring:
        pl.semaphore_signal(barrier, inc=1, device_id=target, device_id_type=MESH)
        greeted += 1
    for n, _, other, _, _ in kinds.values():
        for off in range(1, n):
            pl.semaphore_signal(barrier, inc=1, device_id=other(off)[1], device_id_type=MESH)
            greeted += 1

    sends = []

    def ring_exchange(step, outgoing, incoming):
        copies = []
        for side in range(2):
            copy = pltpu.make_async_remote_copy(
                src_ref=outgoing.at[side],
                dst_ref=incoming.at[1 - side],
                send_sem=ring_send.at[step, side],
                recv_sem=ring_recv.at[step, 1 - side],
                device_id=ring[side],
                device_id_type=MESH,
            )
            copy.start()
            sends.append(copy)
            copies.append(copy)

        def wait():
            for side in range(2):
                pltpu.make_async_remote_copy(
                    src_ref=outgoing.at[1 - side],
                    dst_ref=incoming.at[side],
                    send_sem=ring_send.at[step, 1 - side],
                    recv_sem=ring_recv.at[step, side],
                    device_id=ring[side],
                    device_id_type=MESH,
                ).wait_recv()

        return wait

    def all_to_all(kind, step, outgoing, incoming):
        n, own, other, send, recv = kinds[kind]

        for off in range(1, n):
            j, target = other(off)
            copy = pltpu.make_async_remote_copy(
                src_ref=incoming.at[own] if outgoing is None else outgoing.at[j],
                dst_ref=incoming.at[own],
                send_sem=send.at[step, off],
                recv_sem=recv.at[step, off],
                device_id=target,
                device_id_type=MESH,
            )
            copy.start()
            sends.append(copy)

        def wait():
            for off in range(1, n):
                source, target = other(n - off)
                pltpu.make_async_remote_copy(
                    src_ref=incoming.at[source],
                    dst_ref=incoming.at[source],
                    send_sem=send.at[step, off],
                    recv_sem=recv.at[step, off],
                    device_id=target,
                    device_id_type=MESH,
                ).wait_recv()

        return wait

    loads["rows"].wait()
    for side in range(2):
        listed = jnp.broadcast_to(rows_v[side : side + 1, :], (margin, margin))
        across = lax.broadcasted_iota(jnp.int32, (rows_own, margin), 0)
        spread[:, side * margin : (side + 1) * margin] = (
            across == jnp.broadcast_to(rows_v[side : side + 1, :], (rows_own, margin))
        ).astype(F32).astype(BF16)
        standing = listed.astype(F32).T
        for c in range(row_blocks):
            place = (lax.broadcasted_iota(jnp.int32, (margin, 128), 1) + 128 * c).astype(F32)
            pick[side * margin : (side + 1) * margin, 128 * c : 128 * (c + 1)] = (
                standing == place
            ).astype(F32).astype(BF16)

    def picked_rows(source):
        return dot(pick[...], source).astype(BF16)

    def send_halo(step):
        chosen = picked_rows(rounded[...])
        halo_out[step, 0] = chosen[:margin]
        halo_out[step, 1] = chosen[margin:]
        return ring_exchange(step, halo_out.at[step], halo_in.at[step])

    def inside(vector, target):
        for i in range(row_blocks):
            here = pl.ds(128 * i, 128)
            acc = diag_cols[here, :] * vector[here, :]
            target[here, :] = acc + dot(dense[here, :], rounded[...])

    def across(from_left, from_right):
        return dot(couple_left[...], from_left) + dot(couple_right[...], from_right)

    loads["start"].wait()
    rounded[...] = start[...].astype(BF16)
    loads["cdiag"].wait()
    loads["cup"].wait()
    m1[pos1, 0:8] = pack_block(cdiag[...])
    m1[pos1, 8:16] = pack_block(jnp.where(has_next, cup[...], 0.0))

    chosen = picked_rows(rounded[...])
    halo_out[0, 0] = chosen[:margin]
    halo_out[0, 1] = chosen[margin:]
    pl.semaphore_wait(barrier, greeted)
    wait_m1 = all_to_all("seg", 0, None, m1)
    wait_h1 = ring_exchange(0, halo_out.at[0], halo_in.at[0])

    loads["diag"].wait()
    for i in range(row_blocks):
        standing = jnp.broadcast_to(diag_rows[i : i + 1, :], (128, 128)).T
        diag_cols[128 * i : 128 * (i + 1), 0:128] = standing
        diag_cols[128 * i : 128 * (i + 1), 128:cases] = standing[:, : cases - 128]
    loads["values"].wait()
    for i in range(row_blocks):
        for c in range(row_blocks):
            block = None
            for t in range(values.shape[1]):
                here = (jnp.full((1, 128), cols_ref[i, t], jnp.int32) == c).astype(F32).astype(BF16)
                term = values[i, t] * here
                block = term if block is None else block + term
            dense[128 * i : 128 * (i + 1), 128 * c : 128 * (c + 1)] = block
    inside(start, residual)

    loads["left"].wait()
    loads["right"].wait()
    loads["rhs"].wait()
    wait_h1()
    nothing = jnp.zeros((margin, cases), BF16)
    from_left = jnp.where(has_prev, halo_in[0, 0], nothing)
    from_right = jnp.where(has_next, halo_in[0, 1], nothing)
    residual[...] = rhs[...] - (residual[...] + across(from_left, from_right))
    rounded[...] = residual[...].astype(BF16)
    wait_h2 = send_halo(1)

    wait_m1()
    diag = [unpack_block(m1[i, 0:8]) for i in range(SEG)] + [jnp.zeros((32, 32), F32)]
    up = [unpack_block(m1[i, 8:16]) for i in range(SEG)]
    low = [u.T for u in up]
    d0, u0, _, dn = eliminate(SEG, diag, up, low, f1)
    m2[pos2, 0:8] = pack_block(d0)
    m2[pos2, 8:16] = pack_block(u0)
    m2[pos2, 16:24] = pack_block(dn)
    wait_m2 = all_to_all("mid", 0, None, m2)

    wait_h2()
    extended[0:margin] = jnp.where(has_prev, halo_in[1, 0], nothing)
    extended[margin : margin + rows_own] = rounded[...]
    extended[margin + rows_own :] = jnp.where(has_next, halo_in[1, 1], nothing)
    loads["basis"].wait()
    coarse_in = dot(extended[...], basis[...], 0, 0)
    first_group = [(j * (cases // 8)) // SEG for j in range(SEG)]
    for j in range(SEG):
        at = 8 * first_group[j]
        s1_out[j] = pack_slice(coarse_in[at : at + 8 * SLICE])
    s1[pos1] = s1_out[pos1]
    wait_s1 = all_to_all("seg", 1, s1_out, s1)

    def gathered(n, messages):
        blocks = [[unpack_block(messages[i, 8 * q : 8 * q + 8]) for q in range(3)] for i in range(n)]
        diag = [blocks[0][0]]
        for i in range(1, n):
            diag.append(blocks[i][0] + blocks[i - 1][2])
        return diag + [blocks[n - 1][2]], [b[1] for b in blocks], [b[1].T for b in blocks]

    wait_m2()
    d0, u0, _, dn = eliminate(n2, *gathered(n2, m2), f2)
    m3[grp, 0:8] = pack_block(d0)
    m3[grp, 8:16] = pack_block(u0)
    m3[grp, 16:24] = pack_block(dn)
    wait_m3 = all_to_all("top", 0, None, m3)

    loads["inverse"].wait()

    def local_rows(i, _):
        here = pl.ds(pl.multiple_of(i * 256, 256), 256)
        correction[here, :] = dot(inverse[here, :], extended[...])
        return 0

    lax.fori_loop(0, correction.shape[0] // 256, local_rows, 0)

    def gathered_loads(n, messages):
        a = [unpack_slice(messages[i, 0:8]) for i in range(n)]
        b = [unpack_slice(messages[i, 8:16]) for i in range(n)]
        return [a[0]] + [a[i] + b[i - 1] for i in range(1, n)] + [b[n - 1]]

    wait_s1()
    loads1 = [unpack_slice(s1[i]) for i in range(SEG)] + [jnp.zeros((8 * SLICE, 32), F32)]
    loads1 = sweep_up(SEG, loads1, f1)
    s2[pos2, 0:8] = pack_slice(loads1[0])
    s2[pos2, 8:16] = pack_slice(loads1[SEG])
    wait_s2 = all_to_all("mid", 1, None, s2)
    wait_s2()
    loads2 = sweep_up(n2, gathered_loads(n2, s2), f2)
    s3[grp, 0:8] = pack_slice(loads2[0])
    s3[grp, 8:16] = pack_slice(loads2[n2])
    wait_s3 = all_to_all("top", 1, None, s3)

    wait_m3()
    d0, u0, _, _ = eliminate(n3, *gathered(n3, m3), f3)
    blank = jnp.zeros((32, 32), F32)
    last = gauss_jordan([jnp.concatenate([d0, blank, blank, identity_block()], axis=1)])[0]
    f3[0] = last
    wait_s3()
    loads3 = sweep_up(n3, gathered_loads(n3, s3), f3)
    none = jnp.zeros((8 * SLICE, 32), F32)
    first = dot(jnp.concatenate([none, none, loads3[0], none], axis=1), f3[0], 1, 1, HIGHEST)
    sol3 = sweep_down(n3, loads3, first, none, f3)
    for i in range(n3 + 1):
        x3[i] = sol3[i]
    sol2 = sweep_down(n2, loads2, x3[grp], x3[grp + 1], f2)
    for i in range(n2 + 1):
        x2[i] = sol2[i]
    sol1 = sweep_down(SEG, loads1, x2[pos2], x2[pos2 + 1], f1)
    for j in range(SEG):
        s4_out[j] = pack_slice(sol1[j])
    s4[pos1] = s4_out[pos1]
    wait_s4 = all_to_all("seg", 2, s4_out, s4)
    wait_s4()
    pieces = []
    for group in range(cases // 8):
        j = [j for j in range(SEG) if first_group[j] <= group < first_group[j] + SLICE][0]
        q = group - first_group[j]
        pieces.append(s4[j][:, 32 * q : 32 * q + 32])
    coarse_sol = jnp.concatenate(pieces, axis=0).astype(BF16)

    correction[...] = correction[...] + dot(basis[...], coarse_sol, 1, 1)
    chosen = picked_rows(correction[margin : margin + rows_own].astype(BF16))
    edge_out[0, 0:margin] = correction[0:margin].astype(BF16)
    edge_out[1, 0:margin] = correction[margin + rows_own :].astype(BF16)
    edge_out[0, margin:] = chosen[:margin]
    edge_out[1, margin:] = chosen[margin:]
    wait_edge = ring_exchange(2, edge_out, edge_in)
    wait_edge()
    owned[...] = (
        correction[margin : margin + rows_own]
        + dot(spread[:, :margin], jnp.where(has_prev, edge_in[0, 0:margin], nothing))
        + dot(spread[:, margin:], jnp.where(has_next, edge_in[1, 0:margin], nothing))
    )
    rounded[...] = owned[...].astype(BF16)
    halo_left = (edge_in[0, margin:].astype(F32) + correction[0:margin]).astype(BF16)
    halo_right = (edge_in[1, margin:].astype(F32) + correction[margin + rows_own :]).astype(BF16)
    inside(owned, image)
    image[...] = image[...] + across(
        jnp.where(has_prev, halo_left, nothing), jnp.where(has_next, halo_right, nothing)
    )

    def tile_of(row):
        padded = jnp.concatenate([row[:, 128:], jnp.zeros((1, 256 - cases), F32)], axis=1)
        return [row[:, :128], padded]

    inner = jnp.sum(residual[...] * owned[...], axis=0, keepdims=True)
    curvature = jnp.sum(owned[...] * image[...], axis=0, keepdims=True)
    part = jnp.concatenate(
        tile_of(inner) + tile_of(curvature) + [jnp.zeros((4, 128), F32)], axis=0
    )
    for kind, buffer, step in (("seg", r1, 3), ("mid", r2, 2), ("top", r3, 2)):
        n, own = kinds[kind][:2]
        buffer[own] = part
        all_to_all(kind, step, None, buffer)()
        part = buffer[0]
        for i in range(1, n):
            part = part + buffer[i]
    ratio = part[0:2] / part[2:4]
    step_size = jnp.concatenate([ratio[0:1, :], ratio[1:2, : cases - 128]], axis=1)
    out_iterate[...] = start[...] + step_size * owned[...]
    out_residual[...] = residual[...] - step_size * image[...]
    for copy in sends:
        copy.wait_send()


def solution(mesh):
    n3 = mesh.shape["grp"]
    n2 = mesh.shape["sub"] // SEG

    def shards(
        right_side,
        iterate_in,
        diagonal,
        block_values,
        block_cols,
        couple_left,
        couple_right,
        send_rows,
        local_inverse,
        coarse_basis,
        coarse_diag,
        coarse_up,
    ):
        rows, cases = right_side.shape
        margin = send_rows.shape[2]
        whole = rows + 2 * margin
        modes = coarse_basis.shape[2]
        blocks, nonzeros, block = block_values.shape[1:4]
        vmem = pltpu.VMEM
        dma = pltpu.SemaphoreType.DMA
        tall = vmem((rows, cases), F32)
        any_space = pl.BlockSpec(memory_space=pl.ANY)
        return pl.pallas_call(
            functools.partial(kernel, n2, n3),
            out_shape=[jax.ShapeDtypeStruct((rows, cases), F32)] * 2,
            in_specs=[pl.BlockSpec(memory_space=pltpu.SMEM)] + [any_space] * 11,
            out_specs=[pl.BlockSpec(memory_space=pltpu.VMEM)] * 2,
            scratch_shapes=[
                tall,
                tall,
                vmem((blocks, 128), F32),
                tall,
                vmem((blocks, nonzeros, block, block), BF16),
                vmem((rows, rows), BF16),
                vmem((rows, margin), BF16),
                vmem((rows, margin), BF16),
                vmem((2, margin), jnp.int32),
                vmem((whole, whole), BF16),
                vmem((whole, modes), BF16),
                vmem((modes, modes), F32),
                vmem((modes, modes), F32),
                vmem((rows, cases), BF16),
                vmem((2 * margin, rows), BF16),
                vmem((rows, 2 * margin), BF16),
                vmem((2, 2, margin, cases), BF16),
                vmem((2, 2, margin, cases), BF16),
                vmem((2, 2 * margin, cases), BF16),
                vmem((2, 2 * margin, cases), BF16),
                tall,
                vmem((whole, cases), BF16),
                vmem((whole, cases), F32),
                tall,
                tall,
                vmem((SEG, 16, 128), F32),
                vmem((n2, 24, 128), F32),
                vmem((n3, 24, 128), F32),
                vmem((SEG, 8, 128), F32),
                vmem((SEG, 8, 128), F32),
                vmem((n2, 16, 128), F32),
                vmem((n3, 16, 128), F32),
                vmem((SEG, 8, 128), F32),
                vmem((SEG, 8, 128), F32),
                vmem((SEG, 32, 128), F32),
                vmem((n2, 32, 128), F32),
                vmem((n3, 32, 128), F32),
                vmem((n2 + 1, 8 * SLICE, 32), F32),
                vmem((n3 + 1, 8 * SLICE, 32), F32),
                vmem((SEG, 8, 128), F32),
                vmem((n2, 8, 128), F32),
                vmem((n3, 8, 128), F32),
                dma((11,)),
                dma((3, 2)),
                dma((3, 2)),
                dma((4, SEG)),
                dma((4, SEG)),
                dma((3, n2)),
                dma((3, n2)),
                dma((3, n3)),
                dma((3, n3)),
            ],
            compiler_params=pltpu.CompilerParams(
                collective_id=0, has_side_effects=True, vmem_limit_bytes=48 * 1024 * 1024
            ),
        )(
            block_cols[0],
            right_side,
            iterate_in,
            diagonal.reshape(blocks, 128),
            block_values,
            couple_left,
            couple_right,
            send_rows,
            local_inverse,
            coarse_basis,
            coarse_diag,
            coarse_up,
        )

    split = ("grp", "sub")
    in_specs = (
        P(split, None),
        P(split, None),
        P(split),
        P(split, None, None, None, None),
        P(split, None, None),
        P(split, None),
        P(split, None),
        P(split, None, None),
        P(split, None, None),
        P(split, None, None),
        P(split, None, None),
        P(split, None, None),
    )
    out_specs = (P(split, None), P(split, None))
    return jax.shard_map(
        shards, mesh=mesh, in_specs=in_specs, out_specs=out_specs, check_vma=False
    )
```

```python
import functools

import jax
import jax.numpy as jnp
from jax import lax
from jax.experimental import pallas as pl
from jax.experimental.pallas import tpu as pltpu
from jax.sharding import PartitionSpec as P

MESH = pl.DeviceIdType.MESH
HIGHEST = lax.Precision.HIGHEST
F32 = jnp.float32
BF16 = jnp.bfloat16
SEG = 8
SLICE = 3


def dot(a, b, ca=1, cb=0, precision=None):
    return lax.dot_general(
        a, b, (((ca,), (cb,)), ((), ())), precision=precision, preferred_element_type=F32
    )


def pack_block(x):
    return jnp.concatenate([x[8 * i : 8 * i + 8] for i in range(4)], axis=1)


def unpack_block(t):
    return jnp.concatenate([t[:, 32 * i : 32 * i + 32] for i in range(4)], axis=0)


def pack_slice(x):
    zeros = jnp.zeros((8, 32), F32)
    return jnp.concatenate([x[8 * i : 8 * i + 8] for i in range(SLICE)] + [zeros], axis=1)


def unpack_slice(t):
    return jnp.concatenate([t[:, 32 * i : 32 * i + 32] for i in range(SLICE)], axis=0)


def reduce_blocks(mats):
    sub = lax.broadcasted_iota(jnp.int32, (8, 128), 0)

    def wide(row):
        return jnp.broadcast_to(row, (8, 128))

    def four(state, q, p):
        g, kept, solved = state
        at = 8 * q + p
        later = range(q if p == 0 else q + 1, 4)
        cols = {
            i: [jnp.broadcast_to(g[i][:, at + j : at + j + 1], (8, 128)) for j in range(4)]
            for i in range(q, 4)
        }
        r0, r1, r2, r3 = [wide(g[q][p + j : p + j + 1, :]) for j in range(4)]

        def entry(i, j):
            return wide(cols[q][j][p + i : p + i + 1, :])

        a00, a01, a11 = entry(0, 0), entry(0, 1), entry(1, 1)
        a02, a03, a12, a13 = entry(0, 2), entry(0, 3), entry(1, 2), entry(1, 3)
        a22, a23, a33 = entry(2, 2), entry(2, 3), entry(3, 3)
        inv = 1.0 / (a00 * a11 - a01 * a01)
        i00, i01, i11 = a11 * inv, -a01 * inv, a00 * inv
        t02, t03 = i00 * a02 + i01 * a12, i00 * a03 + i01 * a13
        t12, t13 = i01 * a02 + i11 * a12, i01 * a03 + i11 * a13
        y0, y1 = i00 * r0 + i01 * r1, i01 * r0 + i11 * r1
        s22 = a22 - a02 * t02 - a12 * t12
        s23 = a23 - a02 * t03 - a12 * t13
        s33 = a33 - a03 * t03 - a13 * t13
        q2, q3 = r2 - a02 * y0 - a12 * y1, r3 - a03 * y0 - a13 * y1
        inv = 1.0 / (s22 * s33 - s23 * s23)
        w2 = (s33 * q2 - s23 * q3) * inv
        w3 = (s22 * q3 - s23 * q2) * inv
        w0 = y0 - t02 * w2 - t03 * w3
        w1 = y1 - t12 * w2 - t13 * w3
        w = (w0, w1, w2, w3)
        kept[q] = g[q] if p == 0 else jnp.where(sub < p, kept[q], g[q])
        for j in range(4):
            solved[q] = w0 if p + j == 0 else jnp.where(sub < p + j, solved[q], w[j])
        for i in later:
            c = cols[i]
            g[i] = g[i] - ((c[0] * w0 + c[1] * w1) + (c[2] * w2 + c[3] * w3))

    states = [([m[8 * i : 8 * i + 8] for i in range(4)], [None] * 4, [None] * 4) for m in mats]
    for q in range(4):
        for p in (0, 4):
            for state in states:
                four(state, q, p)
    return [
        dot(jnp.concatenate(kept, axis=0), jnp.concatenate(solved, axis=0), 0, 0, HIGHEST)
        for _, kept, solved in states
    ]


def levels_of(n):
    nodes = list(range(n))
    levels = []
    while len(nodes) > 1:
        ends = nodes + [n]
        levels.append([(ends[q], ends[q - 1], ends[q + 1]) for q in range(1, len(nodes), 2)])
        nodes = nodes[0::2]
    return levels


def identity_block():
    return (
        lax.broadcasted_iota(jnp.int32, (32, 32), 0) == lax.broadcasted_iota(jnp.int32, (32, 32), 1)
    ).astype(F32)


def eliminate(n, diag, up, low, factors):
    diag, up, low = list(diag), list(up), list(low)
    eye = identity_block()
    for level in levels_of(n):
        augmented = [
            jnp.concatenate([diag[o], low[e], up[o], eye], axis=1) for o, e, _ in level
        ]
        for (o, e, f), full in zip(level, reduce_blocks(augmented)):
            factors[o] = full[96:128]
            diag[e] = diag[e] - full[32:64, 32:64]
            diag[f] = diag[f] - full[64:96, 64:96]
            up[e] = -full[32:64, 64:96]
            low[e] = -full[64:96, 32:64]
    return diag[0], up[0], low[0], diag[n]


def sweep_up(n, loads, factors):
    loads = list(loads)
    for level in levels_of(n):
        for o, e, f in level:
            moved = dot(loads[o], factors[o], 1, 0, HIGHEST)
            loads[e] = loads[e] - moved[:, 32:64]
            loads[f] = loads[f] - moved[:, 64:96]
    return loads


def sweep_down(n, loads, first, last, factors):
    sol = [None] * (n + 1)
    sol[0], sol[n] = first, last
    blank = jnp.zeros_like(first)
    for level in reversed(levels_of(n)):
        for o, e, f in level:
            known = jnp.concatenate([blank, -sol[e], -sol[f], loads[o]], axis=1)
            sol[o] = dot(known, factors[o], 1, 1, HIGHEST)
    return sol


def kernel(
    n2,
    n3,
    cols_ref,
    rhs_hbm,
    start_hbm,
    diag_hbm,
    values_hbm,
    left_hbm,
    right_hbm,
    rows_hbm,
    inverse_hbm,
    basis_hbm,
    cdiag_hbm,
    cup_hbm,
    out_iterate,
    out_residual,
    rhs,
    start,
    diag,
    values,
    couple_left,
    couple_right,
    weights,
    rows_v,
    inverse,
    basis,
    cdiag,
    cup,
    pick,
    spread,
    halo_out,
    halo_in,
    edge_out,
    edge_in,
    residual,
    extended,
    correction,
    m1,
    m2,
    m3,
    s1_out,
    s1,
    s2,
    s3,
    s4_out,
    s4,
    f1,
    f2,
    f3,
    x2,
    x3,
    r1,
    r2,
    load_sem,
    ring_send,
    ring_recv,
    seg_send,
    seg_recv,
    mid_send,
    mid_recv,
    top_send,
    top_recv,
    sub_send,
    sub_recv,
):
    cases, rows_own = start.shape
    margin = rows_v.shape[1]
    row_blocks = rows_own // 128
    own = slice(margin, margin + rows_own)
    after = slice(margin + rows_own, 2 * margin + rows_own)
    grp, sub = lax.axis_index("grp"), lax.axis_index("sub")
    members = n2 * SEG
    pos1, pos2 = lax.rem(sub, SEG), lax.div(sub, SEG)
    rank = grp * members + sub
    total = n3 * members
    sub_next, sub_prev = lax.rem(sub + 1, members), lax.rem(sub + members - 1, members)
    grp_next = lax.rem(grp + (sub + 1) // members, n3)
    grp_prev = lax.rem(grp + n3 - (members - sub) // members, n3)
    ring = [(grp_prev, sub_prev), (grp_next, sub_next)]
    has_prev, has_next = rank > 0, rank < total - 1

    def seg_other(off):
        j = lax.rem(pos1 + off, SEG)
        return j, (grp, pos2 * SEG + j)

    def mid_other(off):
        j = lax.rem(pos2 + off, n2)
        return j, (grp, j * SEG + pos1)

    def top_other(off):
        j = lax.rem(grp + off, n3)
        return j, (j, sub)

    def sub_other(off):
        j = lax.rem(sub + off, members)
        return j, (grp, j)

    kinds = {
        "seg": (SEG, pos1, seg_other, seg_send, seg_recv),
        "mid": (n2, pos2, mid_other, mid_send, mid_recv),
        "top": (n3, grp, top_other, top_send, top_recv),
        "sub": (members, sub, sub_other, sub_send, sub_recv),
    }

    loads = {}
    for name, source, target in (
        ("rows", rows_hbm.at[0], rows_v),
        ("start", start_hbm, start),
        ("cdiag", cdiag_hbm.at[0], cdiag),
        ("cup", cup_hbm.at[0], cup),
        ("values", values_hbm.at[0], values),
        ("left", left_hbm, couple_left),
        ("right", right_hbm, couple_right),
        ("diag", diag_hbm, diag),
        ("rhs", rhs_hbm, rhs),
        ("basis", basis_hbm, basis),
        ("inverse", inverse_hbm.at[0], inverse),
    ):
        copy = pltpu.make_async_copy(source, target, load_sem.at[len(loads)])
        copy.start()
        loads[name] = copy

    barrier = pltpu.get_barrier_semaphore()
    greeted = 0
    for kind in ("sub", "top"):
        n, _, other, _, _ = kinds[kind]
        for off in sorted(range(1, n), key=lambda o: -min(o, n - o)):
            pl.semaphore_signal(barrier, inc=1, device_id=other(off)[1], device_id_type=MESH)
            greeted += 1
    for target in ring:
        pl.semaphore_signal(barrier, inc=1, device_id=target, device_id_type=MESH)
        greeted += 1

    sends = []

    def ring_exchange(step, outgoing, incoming):
        for side in range(2):
            copy = pltpu.make_async_remote_copy(
                src_ref=outgoing.at[side],
                dst_ref=incoming.at[1 - side],
                send_sem=ring_send.at[step, side],
                recv_sem=ring_recv.at[step, 1 - side],
                device_id=ring[side],
                device_id_type=MESH,
            )
            copy.start()
            sends.append(copy)

        def wait():
            for side in range(2):
                pltpu.make_async_remote_copy(
                    src_ref=outgoing.at[1 - side],
                    dst_ref=incoming.at[side],
                    send_sem=ring_send.at[step, 1 - side],
                    recv_sem=ring_recv.at[step, side],
                    device_id=ring[side],
                    device_id_type=MESH,
                ).wait_recv()

        return wait

    def all_to_all(kind, step, outgoing, incoming):
        n, place, other, send, recv = kinds[kind]
        order = sorted(range(1, n), key=lambda o: -min(o, n - o))
        for off in order:
            j, target = other(off)
            copy = pltpu.make_async_remote_copy(
                src_ref=incoming.at[place] if outgoing is None else outgoing.at[j],
                dst_ref=incoming.at[place],
                send_sem=send.at[step, off],
                recv_sem=recv.at[step, off],
                device_id=target,
                device_id_type=MESH,
            )
            copy.start()
            sends.append(copy)

        def wait():
            for off in reversed(order):
                source, target = other(n - off)
                pltpu.make_async_remote_copy(
                    src_ref=incoming.at[source],
                    dst_ref=incoming.at[source],
                    send_sem=send.at[step, off],
                    recv_sem=recv.at[step, off],
                    device_id=target,
                    device_id_type=MESH,
                ).wait_recv()

        return wait

    loads["rows"].wait()
    for side in range(2):
        here = slice(side * margin, (side + 1) * margin)
        row = lax.broadcasted_iota(jnp.int32, (rows_own, margin), 0)
        listed = rows_v[side : side + 1, :]
        spread[:, here] = (row == jnp.broadcast_to(listed, (rows_own, margin))).astype(F32).astype(BF16)

    def picked(source):
        return dot(source, spread[...]).astype(BF16)

    loads["start"].wait()
    extended[:, own] = start[...].astype(BF16)
    loads["cdiag"].wait()
    loads["cup"].wait()
    m1[pos1, 0:8] = pack_block(cdiag[...])
    m1[pos1, 8:16] = pack_block(jnp.where(has_next, cup[...], 0.0))
    chosen = picked(extended[:, own])
    halo_out[0, 0] = chosen[:, :margin]
    halo_out[0, 1] = chosen[:, margin:]

    loads["values"].wait()
    for i in range(row_blocks):
        turned = [values[i, t].T for t in range(values.shape[1])]
        for c in range(row_blocks):
            block = None
            for t, term in enumerate(turned):
                here = (jnp.full((1, 128), cols_ref[t, i], jnp.int32) == c).astype(F32).astype(BF16)
                block = term * here if block is None else block + term * here
            weights[margin + 128 * c : margin + 128 * (c + 1), 128 * i : 128 * (i + 1)] = block
    loads["left"].wait()
    loads["right"].wait()
    for i in range(row_blocks):
        here = slice(128 * i, 128 * (i + 1))
        weights[0:margin, here] = couple_left[here, :].T
        weights[after, here] = couple_right[here, :].T
    for side in range(2):
        standing = jnp.broadcast_to(rows_v[side : side + 1, :], (margin, margin)).astype(F32).T
        for c in range(row_blocks):
            place = (lax.broadcasted_iota(jnp.int32, (margin, 128), 1) + 128 * c).astype(F32)
            pick[side * margin : (side + 1) * margin, 128 * c : 128 * (c + 1)] = (
                standing == place
            ).astype(F32).astype(BF16)

    pl.semaphore_wait(barrier, greeted)
    wait_m1 = all_to_all("seg", 0, None, m1)
    wait_h1 = ring_exchange(0, halo_out.at[0], halo_in.at[0])

    loads["diag"].wait()
    loads["rhs"].wait()
    residual[...] = rhs[...] - (diag[...] * start[...] + dot(extended[:, own], weights[own, :]))
    wait_h1()
    nothing = jnp.zeros((cases, margin), BF16)
    from_left = jnp.where(has_prev, halo_in[0, 0], nothing)
    from_right = jnp.where(has_next, halo_in[0, 1], nothing)
    residual[...] = residual[...] - (
        dot(from_left, weights[0:margin, :]) + dot(from_right, weights[after, :])
    )
    extended[:, own] = residual[...].astype(BF16)
    chosen = picked(extended[:, own])
    halo_out[1, 0] = chosen[:, :margin]
    halo_out[1, 1] = chosen[:, margin:]
    wait_h2 = ring_exchange(1, halo_out.at[1], halo_in.at[1])

    wait_m1()
    cdiags = [unpack_block(m1[i, 0:8]) for i in range(SEG)] + [jnp.zeros((32, 32), F32)]
    ups = [unpack_block(m1[i, 8:16]) for i in range(SEG)]
    d0, u0, _, dn = eliminate(SEG, cdiags, ups, [u.T for u in ups], f1)
    m2[pos2, 0:8] = pack_block(d0)
    m2[pos2, 8:16] = pack_block(u0)
    m2[pos2, 16:24] = pack_block(dn)
    wait_m2 = all_to_all("mid", 0, None, m2)

    wait_h2()
    extended[:, 0:margin] = jnp.where(has_prev, halo_in[1, 0], nothing)
    extended[:, after] = jnp.where(has_next, halo_in[1, 1], nothing)
    loads["basis"].wait()
    coarse_in = dot(extended[...], basis[...], 1, 1)
    first_group = [(j * (cases // 8)) // SEG for j in range(SEG)]
    for j in range(SEG):
        at = 8 * first_group[j]
        s1_out[j] = pack_slice(coarse_in[at : at + 8 * SLICE])
    s1[pos1] = s1_out[pos1]
    wait_s1 = all_to_all("seg", 1, s1_out, s1)

    loads["inverse"].wait()
    for c in range(0, correction.shape[1], 256):
        correction[:, c : c + 256] = dot(extended[...], inverse[:, c : c + 256])

    def gathered(n, messages):
        blocks = [[unpack_block(messages[i, 8 * q : 8 * q + 8]) for q in range(3)] for i in range(n)]
        summed = [blocks[0][0]]
        for i in range(1, n):
            summed.append(blocks[i][0] + blocks[i - 1][2])
        return summed + [blocks[n - 1][2]], [b[1] for b in blocks], [b[1].T for b in blocks]

    def gathered_loads(n, messages):
        a = [unpack_slice(messages[i, 0:8]) for i in range(n)]
        b = [unpack_slice(messages[i, 8:16]) for i in range(n)]
        return [a[0]] + [a[i] + b[i - 1] for i in range(1, n)] + [b[n - 1]]

    wait_s1()
    loads1 = [unpack_slice(s1[i]) for i in range(SEG)] + [jnp.zeros((8 * SLICE, 32), F32)]
    loads1 = sweep_up(SEG, loads1, f1)
    s2[pos2, 0:8] = pack_slice(loads1[0])
    s2[pos2, 8:16] = pack_slice(loads1[SEG])
    wait_s2 = all_to_all("mid", 1, None, s2)

    wait_m2()
    d0, u0, _, dn = eliminate(n2, *gathered(n2, m2), f2)
    m3[grp, 0:8] = pack_block(d0)
    m3[grp, 8:16] = pack_block(u0)
    m3[grp, 16:24] = pack_block(dn)
    wait_m3 = all_to_all("top", 0, None, m3)
    wait_s2()
    loads2 = sweep_up(n2, gathered_loads(n2, s2), f2)
    s3[grp, 0:8] = pack_slice(loads2[0])
    s3[grp, 8:16] = pack_slice(loads2[n2])
    wait_s3 = all_to_all("top", 1, None, s3)

    wait_m3()
    d0, u0, _, _ = eliminate(n3, *gathered(n3, m3), f3)
    blank = jnp.zeros((32, 32), F32)
    augmented = jnp.concatenate([d0, blank, blank, identity_block()], axis=1)
    f3[0] = reduce_blocks([augmented])[0][96:128]
    wait_s3()
    loads3 = sweep_up(n3, gathered_loads(n3, s3), f3)
    none = jnp.zeros((8 * SLICE, 32), F32)
    first = dot(jnp.concatenate([none, none, none, loads3[0]], axis=1), f3[0], 1, 1, HIGHEST)
    sol3 = sweep_down(n3, loads3, first, none, f3)
    for i in range(n3 + 1):
        x3[i] = sol3[i]
    sol2 = sweep_down(n2, loads2, x3[grp], x3[grp + 1], f2)
    for i in range(n2 + 1):
        x2[i] = sol2[i]
    sol1 = sweep_down(SEG, loads1, x2[pos2], x2[pos2 + 1], f1)
    for j in range(SEG):
        s4_out[j] = pack_slice(sol1[j])
    s4[pos1] = s4_out[pos1]
    wait_s4 = all_to_all("seg", 2, s4_out, s4)
    wait_s4()
    pieces = []
    for group in range(cases // 8):
        j = [j for j in range(SEG) if first_group[j] <= group < first_group[j] + SLICE][0]
        q = group - first_group[j]
        pieces.append(s4[j][:, 32 * q : 32 * q + 32])
    coarse_sol = jnp.concatenate(pieces, axis=0).astype(BF16)

    correction[...] = correction[...] + dot(coarse_sol, basis[...])
    chosen = picked(correction[:, own].astype(BF16))
    edge_out[0, :, 0:margin] = correction[:, 0:margin].astype(BF16)
    edge_out[1, :, 0:margin] = correction[:, after].astype(BF16)
    edge_out[0, :, margin:] = chosen[:, :margin]
    edge_out[1, :, margin:] = chosen[:, margin:]
    wait_edge = ring_exchange(2, edge_out, edge_in)
    wait_edge()
    extended[:, 0:margin] = jnp.where(has_prev, edge_in[0, :, 0:margin], nothing)
    extended[:, margin : 2 * margin] = jnp.where(has_next, edge_in[1, :, 0:margin], nothing)
    owned = correction[:, own] + dot(extended[:, 0 : 2 * margin], pick[...])
    before = (edge_in[0, :, margin:].astype(F32) + correction[:, 0:margin]).astype(BF16)
    beyond = (edge_in[1, :, margin:].astype(F32) + correction[:, after]).astype(BF16)
    correction[:, own] = owned
    extended[:, own] = owned.astype(BF16)
    extended[:, 0:margin] = jnp.where(has_prev, before, nothing)
    extended[:, after] = jnp.where(has_next, beyond, nothing)
    image = diag[...] * correction[:, own] + dot(extended[...], weights[...])
    out_residual[...] = image

    def column_sums(x):
        total = x[:, 0:128]
        for i in range(1, row_blocks):
            total = total + x[:, 128 * i : 128 * (i + 1)]
        row = jnp.sum(total.T, axis=0, keepdims=True)
        rest = jnp.concatenate([row[:, 128:cases], jnp.zeros((1, 256 - cases), F32)], axis=1)
        return [row[:, 0:128], rest]

    inner = column_sums(residual[...] * correction[:, own])
    curvature = column_sums(correction[:, own] * out_residual[...])
    part = jnp.concatenate(inner + curvature, axis=0)
    for kind, buffer, step in (("sub", r1, 0), ("top", r2, 2)):
        n, place = kinds[kind][:2]
        buffer[place] = part
        all_to_all(kind, step, None, buffer)()
        part = buffer[0]
        for i in range(1, n):
            part = part + buffer[i]
    ratio = part[0:2] / part[2:4]
    step_row = jnp.concatenate([ratio[0:1, :], ratio[1:2, : cases - 128]], axis=1)
    step_size = jnp.broadcast_to(step_row, (8, cases)).T[:, 0:1]
    out_iterate[...] = start[...] + step_size * correction[:, own]
    out_residual[...] = residual[...] - step_size * out_residual[...]
    for copy in sends:
        copy.wait_send()


def solution(mesh):
    n3 = mesh.shape["grp"]
    n2 = mesh.shape["sub"] // SEG

    def shards(
        right_side,
        iterate_in,
        diagonal,
        block_values,
        block_cols,
        couple_left,
        couple_right,
        send_rows,
        local_inverse,
        coarse_basis,
        coarse_diag,
        coarse_up,
    ):
        rows, cases = right_side.shape
        margin = send_rows.shape[2]
        whole = rows + 2 * margin
        modes = coarse_basis.shape[2]
        blocks, nonzeros, block = block_values.shape[1:4]
        members = n2 * SEG
        vmem = pltpu.VMEM
        dma = pltpu.SemaphoreType.DMA
        flat = vmem((cases, rows), F32)
        any_space = pl.BlockSpec(memory_space=pl.ANY)
        outs = pl.pallas_call(
            functools.partial(kernel, n2, n3),
            out_shape=[jax.ShapeDtypeStruct((cases, rows), F32)] * 2,
            in_specs=[pl.BlockSpec(memory_space=pltpu.SMEM)] + [any_space] * 11,
            out_specs=[pl.BlockSpec(memory_space=pltpu.VMEM)] * 2,
            scratch_shapes=[
                flat,
                flat,
                vmem((1, rows), F32),
                vmem((blocks, nonzeros, block, block), BF16),
                vmem((rows, margin), BF16),
                vmem((rows, margin), BF16),
                vmem((whole, rows), BF16),
                vmem((2, margin), jnp.int32),
                vmem((whole, whole), BF16),
                vmem((modes, whole), BF16),
                vmem((modes, modes), F32),
                vmem((modes, modes), F32),
                vmem((2 * margin, rows), BF16),
                vmem((rows, 2 * margin), BF16),
                vmem((2, 2, cases, margin), BF16),
                vmem((2, 2, cases, margin), BF16),
                vmem((2, cases, 2 * margin), BF16),
                vmem((2, cases, 2 * margin), BF16),
                flat,
                vmem((cases, whole), BF16),
                vmem((cases, whole), F32),
                vmem((SEG, 16, 128), F32),
                vmem((n2, 24, 128), F32),
                vmem((n3, 24, 128), F32),
                vmem((SEG, 8, 128), F32),
                vmem((SEG, 8, 128), F32),
                vmem((n2, 16, 128), F32),
                vmem((n3, 16, 128), F32),
                vmem((SEG, 8, 128), F32),
                vmem((SEG, 8, 128), F32),
                vmem((SEG, 32, 128), F32),
                vmem((n2, 32, 128), F32),
                vmem((n3, 32, 128), F32),
                vmem((n2 + 1, 8 * SLICE, 32), F32),
                vmem((n3 + 1, 8 * SLICE, 32), F32),
                vmem((members, 4, 128), F32),
                vmem((n3, 4, 128), F32),
                dma((11,)),
                dma((3, 2)),
                dma((3, 2)),
                dma((3, SEG)),
                dma((3, SEG)),
                dma((2, n2)),
                dma((2, n2)),
                dma((3, n3)),
                dma((3, n3)),
                dma((1, members)),
                dma((1, members)),
            ],
            compiler_params=pltpu.CompilerParams(
                collective_id=0, has_side_effects=True, vmem_limit_bytes=60 * 1024 * 1024
            ),
        )(
            block_cols[0].T,
            right_side.T,
            iterate_in.T,
            diagonal.reshape(1, rows),
            block_values,
            couple_left,
            couple_right,
            send_rows,
            local_inverse,
            coarse_basis[0].T,
            coarse_diag,
            coarse_up,
        )
        return tuple(out.T for out in outs)

    split = ("grp", "sub")
    in_specs = (
        P(split, None),
        P(split, None),
        P(split),
        P(split, None, None, None, None),
        P(split, None, None),
        P(split, None),
        P(split, None),
        P(split, None, None),
        P(split, None, None),
        P(split, None, None),
        P(split, None, None),
        P(split, None, None),
    )
    out_specs = (P(split, None), P(split, None))
    return jax.shard_map(
        shards, mesh=mesh, in_specs=in_specs, out_specs=out_specs, check_vma=False
    )
```

```python
import functools

import jax
import jax.numpy as jnp
from jax import lax
from jax.experimental import pallas as pl
from jax.experimental.pallas import tpu as pltpu
from jax.sharding import PartitionSpec as P

MESH = pl.DeviceIdType.MESH
HIGHEST = lax.Precision.HIGHEST
F32 = jnp.float32
BF16 = jnp.bfloat16
SEG = 8
PARTS = 2
SLICE = 3


def dot(a, b, ca=1, cb=0, precision=None):
    return lax.dot_general(
        a, b, (((ca,), (cb,)), ((), ())), precision=precision, preferred_element_type=F32
    )


def pack_block(x):
    return jnp.concatenate([x[8 * i : 8 * i + 8] for i in range(4)], axis=1)


def unpack_block(t):
    return jnp.concatenate([t[:, 32 * i : 32 * i + 32] for i in range(4)], axis=0)


def pack_slice(x):
    zeros = jnp.zeros((8, 32), F32)
    return jnp.concatenate([x[8 * i : 8 * i + 8] for i in range(SLICE)] + [zeros], axis=1)


def unpack_slice(t):
    return jnp.concatenate([t[:, 32 * i : 32 * i + 32] for i in range(SLICE)], axis=0)


def reduce_blocks(mats):
    sub = lax.broadcasted_iota(jnp.int32, (8, 128), 0)

    def wide(row):
        return jnp.broadcast_to(row, (8, 128))

    def four(state, q, p):
        g, kept, solved = state
        at = 8 * q + p
        later = range(q if p == 0 else q + 1, 4)
        cols = {
            i: [jnp.broadcast_to(g[i][:, at + j : at + j + 1], (8, 128)) for j in range(4)]
            for i in range(q, 4)
        }
        r0, r1, r2, r3 = [wide(g[q][p + j : p + j + 1, :]) for j in range(4)]

        def entry(i, j):
            return wide(cols[q][j][p + i : p + i + 1, :])

        a00, a01, a11 = entry(0, 0), entry(0, 1), entry(1, 1)
        a02, a03, a12, a13 = entry(0, 2), entry(0, 3), entry(1, 2), entry(1, 3)
        a22, a23, a33 = entry(2, 2), entry(2, 3), entry(3, 3)
        inv = 1.0 / (a00 * a11 - a01 * a01)
        i00, i01, i11 = a11 * inv, -a01 * inv, a00 * inv
        t02, t03 = i00 * a02 + i01 * a12, i00 * a03 + i01 * a13
        t12, t13 = i01 * a02 + i11 * a12, i01 * a03 + i11 * a13
        y0, y1 = i00 * r0 + i01 * r1, i01 * r0 + i11 * r1
        s22 = a22 - a02 * t02 - a12 * t12
        s23 = a23 - a02 * t03 - a12 * t13
        s33 = a33 - a03 * t03 - a13 * t13
        q2, q3 = r2 - a02 * y0 - a12 * y1, r3 - a03 * y0 - a13 * y1
        inv = 1.0 / (s22 * s33 - s23 * s23)
        w2 = (s33 * q2 - s23 * q3) * inv
        w3 = (s22 * q3 - s23 * q2) * inv
        w0 = y0 - t02 * w2 - t03 * w3
        w1 = y1 - t12 * w2 - t13 * w3
        w = (w0, w1, w2, w3)
        kept[q] = g[q] if p == 0 else jnp.where(sub < p, kept[q], g[q])
        for j in range(4):
            solved[q] = w0 if p + j == 0 else jnp.where(sub < p + j, solved[q], w[j])
        for i in later:
            c = cols[i]
            g[i] = g[i] - ((c[0] * w0 + c[1] * w1) + (c[2] * w2 + c[3] * w3))

    states = [([m[8 * i : 8 * i + 8] for i in range(4)], [None] * 4, [None] * 4) for m in mats]
    for q in range(4):
        for p in (0, 4):
            for state in states:
                four(state, q, p)
    return [
        dot(jnp.concatenate(kept, axis=0), jnp.concatenate(solved, axis=0), 0, 0, HIGHEST)
        for _, kept, solved in states
    ]


def levels_of(n):
    nodes = list(range(n))
    levels = []
    while len(nodes) > 1:
        ends = nodes + [n]
        levels.append([(ends[q], ends[q - 1], ends[q + 1]) for q in range(1, len(nodes), 2)])
        nodes = nodes[0::2]
    return levels


def identity_block():
    return (
        lax.broadcasted_iota(jnp.int32, (32, 32), 0) == lax.broadcasted_iota(jnp.int32, (32, 32), 1)
    ).astype(F32)


def products(inverse, augmented):
    return dot(augmented, dot(inverse, augmented, 1, 0, HIGHEST), 0, 0, HIGHEST)


def eliminate(n, diag, up, low, factors, loads=None, inverses=None):
    diag, up, low = list(diag), list(up), list(low)
    eye = identity_block()
    for depth, level in enumerate(levels_of(n)):
        known = inverses is not None and depth == 0
        first = jnp.zeros((32, 32), F32)
        augmented = [
            jnp.concatenate([first if known else diag[o], low[e], up[o], eye], axis=1)
            for o, e, _ in level
        ]
        if known:
            reduced = [products(inverses[o], m) for (o, _, _), m in zip(level, augmented)]
        else:
            reduced = reduce_blocks(augmented)
        for (o, e, f), full in zip(level, reduced):
            factors[o] = full[96:128]
            diag[e] = diag[e] - full[32:64, 32:64]
            diag[f] = diag[f] - full[64:96, 64:96]
            up[e] = -full[32:64, 64:96]
            low[e] = -full[64:96, 32:64]
            if loads is not None:
                moved = dot(loads[o], full[96:128], 1, 0, HIGHEST)
                loads[e] = loads[e] - moved[:, 32:64]
                loads[f] = loads[f] - moved[:, 64:96]
    return diag[0], up[0], low[0], diag[n]


def sweep_up(n, loads, factors):
    loads = list(loads)
    for level in levels_of(n):
        for o, e, f in level:
            moved = dot(loads[o], factors[o], 1, 0, HIGHEST)
            loads[e] = loads[e] - moved[:, 32:64]
            loads[f] = loads[f] - moved[:, 64:96]
    return loads


def sweep_down(n, loads, first, last, factors):
    sol = [None] * (n + 1)
    sol[0], sol[n] = first, last
    blank = jnp.zeros_like(first)
    for level in reversed(levels_of(n)):
        for o, e, f in level:
            known = jnp.concatenate([blank, -sol[e], -sol[f], loads[o]], axis=1)
            sol[o] = dot(known, factors[o], 1, 1, HIGHEST)
    return sol


def response(n, loads, factors):
    eye, rows = identity_block(), loads[0].shape[0]
    none, short = jnp.zeros((32, 32), F32), jnp.zeros((rows, 32), F32)
    first = jnp.concatenate([eye, none, short], axis=0)
    last = jnp.concatenate([none, eye, short], axis=0)
    padded = [jnp.concatenate([none, none, x], axis=0) for x in loads]
    return sweep_down(n, padded, first, last, factors)


def kernel(
    n2,
    n3,
    cols_ref,
    rhs_hbm,
    start_hbm,
    diag_hbm,
    values_hbm,
    left_hbm,
    right_hbm,
    rows_hbm,
    inverse_hbm,
    basis_hbm,
    cdiag_hbm,
    cup_hbm,
    out_step,
    out_direction,
    out_image,
    out_start,
    rhs,
    start,
    diag_rows,
    diag,
    values,
    couple_left,
    couple_right,
    weights,
    rows_v,
    inverse,
    basis,
    cdiag,
    cup,
    pick,
    spread,
    halo_out,
    halo_in,
    edge_out,
    edge_in,
    residual,
    extended,
    correction,
    image,
    m1,
    m2,
    m3,
    s1_out,
    s1,
    s2,
    s3,
    s4_out,
    s4,
    f1,
    f2,
    f3,
    reply,
    x2,
    x3,
    r1,
    r2,
    load_sem,
    store_sem,
    ring_send,
    ring_recv,
    seg_send,
    seg_recv,
    mid_send,
    mid_recv,
    top_send,
    top_recv,
    sub_send,
    sub_recv,
):
    cases, rows_own = start.shape
    margin = rows_v.shape[1]
    row_blocks = rows_own // 128
    own = slice(margin, margin + rows_own)
    after = slice(margin + rows_own, 2 * margin + rows_own)
    grp, sub = lax.axis_index("grp"), lax.axis_index("sub")
    members = n2 * SEG
    pos1, pos2 = lax.rem(sub, SEG), lax.div(sub, SEG)
    rank = grp * members + sub
    total = n3 * members
    sub_next, sub_prev = lax.rem(sub + 1, members), lax.rem(sub + members - 1, members)
    grp_next = lax.rem(grp + (sub + 1) // members, n3)
    grp_prev = lax.rem(grp + n3 - (members - sub) // members, n3)
    ring = [(grp_prev, sub_prev), (grp_next, sub_next)]
    has_prev, has_next = rank > 0, rank < total - 1

    def seg_other(off):
        j = lax.rem(pos1 + off, SEG)
        return j, (grp, pos2 * SEG + j)

    def mid_other(off):
        j = lax.rem(pos2 + off, n2)
        return j, (grp, j * SEG + pos1)

    def top_other(off):
        j = lax.rem(grp + off, n3)
        return j, (j, sub)

    def sub_other(off):
        j = lax.rem(sub + off, members)
        return j, (grp, j)

    kinds = {
        "seg": (SEG, pos1, seg_other, seg_send, seg_recv),
        "mid": (n2, pos2, mid_other, mid_send, mid_recv),
        "top": (n3, grp, top_other, top_send, top_recv),
        "sub": (members, sub, sub_other, sub_send, sub_recv),
    }

    loads = {}
    for name, source, target in (
        ("rows", rows_hbm.at[0], rows_v),
        ("start", start_hbm, start),
        ("cdiag", cdiag_hbm.at[0], cdiag),
        ("cup", cup_hbm.at[0], cup),
        ("values", values_hbm.at[0], values),
        ("left", left_hbm, couple_left),
        ("right", right_hbm, couple_right),
        ("diag", diag_hbm, diag_rows),
        ("rhs", rhs_hbm, rhs),
        ("basis", basis_hbm, basis),
        ("inverse", inverse_hbm.at[0], inverse),
    ):
        copy = pltpu.make_async_copy(source, target, load_sem.at[len(loads)])
        copy.start()
        loads[name] = copy

    barrier = pltpu.get_barrier_semaphore()
    greeted = 0
    for kind in ("sub", "top"):
        n, _, other, _, _ = kinds[kind]
        for off in sorted(range(1, n), key=lambda o: -min(o, n - o)):
            pl.semaphore_signal(barrier, inc=1, device_id=other(off)[1], device_id_type=MESH)
            greeted += 1
    for target in ring:
        pl.semaphore_signal(barrier, inc=1, device_id=target, device_id_type=MESH)
        greeted += 1

    sends = []

    def ring_exchange(step, outgoing, incoming):
        for side in range(2):
            copy = pltpu.make_async_remote_copy(
                src_ref=outgoing.at[side],
                dst_ref=incoming.at[1 - side],
                send_sem=ring_send.at[step, side],
                recv_sem=ring_recv.at[step, 1 - side],
                device_id=ring[side],
                device_id_type=MESH,
            )
            copy.start()
            sends.append(copy)

        def wait():
            for side in range(2):
                pltpu.make_async_remote_copy(
                    src_ref=outgoing.at[1 - side],
                    dst_ref=incoming.at[side],
                    send_sem=ring_send.at[step, 1 - side],
                    recv_sem=ring_recv.at[step, side],
                    device_id=ring[side],
                    device_id_type=MESH,
                ).wait_recv()

        return wait

    def all_to_all(kind, step, outgoing, incoming):
        n, place, other, send, recv = kinds[kind]
        order = sorted(range(1, n), key=lambda o: -min(o, n - o))
        for off in order:
            j, target = other(off)
            copy = pltpu.make_async_remote_copy(
                src_ref=incoming.at[place] if outgoing is None else outgoing.at[j],
                dst_ref=incoming.at[place],
                send_sem=send.at[step, off],
                recv_sem=recv.at[step, off],
                device_id=target,
                device_id_type=MESH,
            )
            copy.start()
            sends.append(copy)

        def wait():
            for off in reversed(order):
                source, target = other(n - off)
                pltpu.make_async_remote_copy(
                    src_ref=incoming.at[source],
                    dst_ref=incoming.at[source],
                    send_sem=send.at[step, off],
                    recv_sem=recv.at[step, off],
                    device_id=target,
                    device_id_type=MESH,
                ).wait_recv()

        return wait

    loads["rows"].wait()
    for side in range(2):
        here = slice(side * margin, (side + 1) * margin)
        row = lax.broadcasted_iota(jnp.int32, (rows_own, margin), 0)
        listed = rows_v[side : side + 1, :]
        spread[:, here] = (row == jnp.broadcast_to(listed, (rows_own, margin))).astype(F32).astype(BF16)

    def picked(source):
        return dot(source, spread[...]).astype(BF16)

    loads["start"].wait()
    extended[:, own] = start[...].astype(BF16)
    loads["cdiag"].wait()
    loads["cup"].wait()
    blank = jnp.zeros((32, 32), F32)
    augmented = jnp.concatenate([cdiag[...], blank, blank, identity_block()], axis=1)
    m1[pos1, 16:24] = pack_block(reduce_blocks([augmented])[0][96:128, 96:128])
    m1[pos1, 0:8] = pack_block(cdiag[...])
    m1[pos1, 8:16] = pack_block(jnp.where(has_next, cup[...], 0.0))
    chosen = picked(extended[:, own])
    halo_out[0, 0] = chosen[:, :margin]
    halo_out[0, 1] = chosen[:, margin:]

    loads["values"].wait()
    for i in range(row_blocks):
        turned = [values[i, t].T for t in range(values.shape[1])]
        for c in range(row_blocks):
            block = None
            for t, term in enumerate(turned):
                here = (jnp.full((1, 128), cols_ref[t, 0, i], jnp.int32) == c).astype(F32).astype(BF16)
                block = term * here if block is None else block + term * here
            weights[margin + 128 * c : margin + 128 * (c + 1), 128 * i : 128 * (i + 1)] = block
    loads["left"].wait()
    loads["right"].wait()
    for i in range(row_blocks):
        here = slice(128 * i, 128 * (i + 1))
        weights[0:margin, here] = couple_left[here, :].T
        weights[after, here] = couple_right[here, :].T
    for side in range(2):
        standing = jnp.broadcast_to(rows_v[side : side + 1, :], (margin, margin)).astype(F32).T
        for c in range(row_blocks):
            place = (lax.broadcasted_iota(jnp.int32, (margin, 128), 1) + 128 * c).astype(F32)
            pick[side * margin : (side + 1) * margin, 128 * c : 128 * (c + 1)] = (
                standing == place
            ).astype(F32).astype(BF16)

    pl.semaphore_wait(barrier, greeted)
    wait_m1 = all_to_all("seg", 0, None, m1)
    wait_h1 = ring_exchange(0, halo_out.at[0], halo_in.at[0])

    loads["diag"].wait()
    for i in range(row_blocks):
        diag[:, 128 * i : 128 * (i + 1)] = diag_rows[i : i + 1, :]
    loads["rhs"].wait()
    residual[...] = rhs[...] - (diag[...] * start[...] + dot(extended[:, own], weights[own, :]))
    wait_h1()
    nothing = jnp.zeros((cases, margin), BF16)
    from_left = jnp.where(has_prev, halo_in[0, 0], nothing)
    from_right = jnp.where(has_next, halo_in[0, 1], nothing)
    residual[...] = residual[...] - (
        dot(from_left, weights[0:margin, :]) + dot(from_right, weights[after, :])
    )
    extended[:, own] = residual[...].astype(BF16)
    chosen = picked(extended[:, own])
    halo_out[1, 0] = chosen[:, :margin]
    halo_out[1, 1] = chosen[:, margin:]
    wait_h2 = ring_exchange(1, halo_out.at[1], halo_in.at[1])

    wait_m1()
    cdiags = [unpack_block(m1[i, 0:8]) for i in range(SEG)] + [jnp.zeros((32, 32), F32)]
    ups = [unpack_block(m1[i, 8:16]) for i in range(SEG)]
    inverses = [unpack_block(m1[i, 16:24]) for i in range(SEG)]
    d0, u0, _, dn = eliminate(SEG, cdiags, ups, [u.T for u in ups], f1, None, inverses)
    m2[pos2, 0:8] = pack_block(d0)
    m2[pos2, 8:16] = pack_block(u0)
    m2[pos2, 16:24] = pack_block(dn)
    wait_m2 = all_to_all("mid", 0, None, m2)

    wait_h2()
    extended[:, 0:margin] = jnp.where(has_prev, halo_in[1, 0], nothing)
    extended[:, after] = jnp.where(has_next, halo_in[1, 1], nothing)
    loads["basis"].wait()
    coarse_in = dot(extended[...], basis[...], 1, 1)
    first_group = [(j * (cases // 8)) // SEG for j in range(SEG)]
    for j in range(SEG):
        at = 8 * first_group[j]
        s1_out[j] = pack_slice(coarse_in[at : at + 8 * SLICE])
    s1[pos1] = s1_out[pos1]
    wait_s1 = all_to_all("seg", 1, s1_out, s1)

    loads["inverse"].wait()
    for c in range(0, correction.shape[1], 256):
        correction[:, c : c + 256] = dot(extended[...], inverse[:, c : c + 256])

    def gathered(n, messages):
        blocks = [[unpack_block(messages[i, 8 * q : 8 * q + 8]) for q in range(3)] for i in range(n)]
        summed = [blocks[0][0]]
        for i in range(1, n):
            summed.append(blocks[i][0] + blocks[i - 1][2])
        return summed + [blocks[n - 1][2]], [b[1] for b in blocks], [b[1].T for b in blocks]

    def gathered_loads(n, messages):
        a = [unpack_slice(messages[i, 0:8]) for i in range(n)]
        b = [unpack_slice(messages[i, 8:16]) for i in range(n)]
        return [a[0]] + [a[i] + b[i - 1] for i in range(1, n)] + [b[n - 1]]

    wait_s1()
    loads1 = [unpack_slice(s1[i]) for i in range(SEG)] + [jnp.zeros((8 * SLICE, 32), F32)]
    loads1 = sweep_up(SEG, loads1, f1)
    s2[pos2, 0:8] = pack_slice(loads1[0])
    s2[pos2, 8:16] = pack_slice(loads1[SEG])
    wait_s2 = all_to_all("mid", 1, None, s2)
    reply1 = response(SEG, loads1, f1)
    for i in range(SEG):
        reply[:, 32 * i : 32 * i + 32] = reply1[i]

    wait_m2()
    d0, u0, _, dn = eliminate(n2, *gathered(n2, m2), f2)
    m3[grp, 0:8] = pack_block(d0)
    m3[grp, 8:16] = pack_block(u0)
    m3[grp, 16:24] = pack_block(dn)
    wait_m3 = all_to_all("top", 0, None, m3)
    wait_s2()
    loads2 = sweep_up(n2, gathered_loads(n2, s2), f2)
    s3[grp, 0:8] = pack_slice(loads2[0])
    s3[grp, 8:16] = pack_slice(loads2[n2])
    wait_s3 = all_to_all("top", 1, None, s3)
    reply2 = response(n2, loads2, f2)
    for i in range(n2 + 1):
        x2[i] = reply2[i]
    ends = jnp.concatenate([x2[pos2], x2[pos2 + 1]], axis=1)
    through = dot(ends, reply[0:64], 1, 0, HIGHEST)
    reply[0:64] = through[0:64]
    reply[64:] = through[64:] + reply[64:]

    wait_m3()
    wait_s3()
    loads3 = gathered_loads(n3, s3)
    d0, u0, _, _ = eliminate(n3, *gathered(n3, m3), f3, loads3)
    augmented = jnp.concatenate([d0, blank, blank, identity_block()], axis=1)
    f3[0] = reduce_blocks([augmented])[0][96:128]
    none = jnp.zeros((8 * SLICE, 32), F32)
    first = dot(jnp.concatenate([none, none, none, loads3[0]], axis=1), f3[0], 1, 1, HIGHEST)
    sol3 = sweep_down(n3, loads3, first, none, f3)
    for i in range(n3 + 1):
        x3[i] = sol3[i]
    ends = jnp.concatenate([x3[grp], x3[grp + 1]], axis=1)
    sol1 = dot(ends, reply[0:64], 1, 0, HIGHEST) + reply[64:]
    for j in range(SEG):
        s4_out[j] = pack_slice(sol1[:, 32 * j : 32 * j + 32])
    s4[pos1] = s4_out[pos1]
    wait_s4 = all_to_all("seg", 2, s4_out, s4)
    wait_s4()
    pieces = []
    for group in range(cases // 8):
        j = [j for j in range(SEG) if first_group[j] <= group < first_group[j] + SLICE][0]
        q = group - first_group[j]
        pieces.append(s4[j][:, 32 * q : 32 * q + 32])
    coarse_sol = jnp.concatenate(pieces, axis=0).astype(BF16)

    correction[...] = correction[...] + dot(coarse_sol, basis[...])
    chosen = picked(correction[:, own].astype(BF16))
    edge_out[0, :, 0:margin] = correction[:, 0:margin].astype(BF16)
    edge_out[1, :, 0:margin] = correction[:, after].astype(BF16)
    edge_out[0, :, margin:] = chosen[:, :margin]
    edge_out[1, :, margin:] = chosen[:, margin:]
    wait_edge = ring_exchange(2, edge_out, edge_in)
    wait_edge()
    extended[:, 0:margin] = jnp.where(has_prev, edge_in[0, :, 0:margin], nothing)
    extended[:, margin : 2 * margin] = jnp.where(has_next, edge_in[1, :, 0:margin], nothing)
    owned = correction[:, own] + dot(extended[:, 0 : 2 * margin], pick[...])
    before = (edge_in[0, :, margin:].astype(F32) + correction[:, 0:margin]).astype(BF16)
    beyond = (edge_in[1, :, margin:].astype(F32) + correction[:, after]).astype(BF16)
    correction[:, own] = owned
    extended[:, own] = owned.astype(BF16)
    extended[:, 0:margin] = jnp.where(has_prev, before, nothing)
    extended[:, after] = jnp.where(has_next, beyond, nothing)
    image[...] = diag[...] * correction[:, own] + dot(extended[...], weights[...])
    stores = []
    for source, target in (
        (correction.at[:, own], out_direction),
        (image, out_image),
        (residual, out_start),
    ):
        stores.append(pltpu.make_async_copy(source, target, store_sem.at[len(stores)]))
        stores[-1].start()

    def column_sums(x):
        total = x[:, 0:128]
        for i in range(1, row_blocks):
            total = total + x[:, 128 * i : 128 * (i + 1)]
        row = jnp.sum(total.T, axis=0, keepdims=True)
        rest = jnp.concatenate([row[:, 128:cases], jnp.zeros((1, 256 - cases), F32)], axis=1)
        return [row[:, 0:128], rest]

    inner = column_sums(residual[...] * correction[:, own])
    curvature = column_sums(correction[:, own] * image[...])
    part = jnp.concatenate(inner + curvature, axis=0)
    for kind, buffer, step in (("sub", r1, 0), ("top", r2, 2)):
        n, place = kinds[kind][:2]
        buffer[place] = part
        all_to_all(kind, step, None, buffer)()
        part = buffer[0]
        for i in range(1, n):
            part = part + buffer[i]
    ratio = part[0:2] / part[2:4]
    step_row = jnp.concatenate([ratio[0:1, :], ratio[1:2, : cases - 128]], axis=1)
    out_step[...] = jnp.broadcast_to(step_row, (128, cases)).T
    for copy in stores:
        copy.wait()
    for copy in sends:
        copy.wait_send()


def update(step, start, direction, residual, image, out_iterate, out_residual):
    wide = jnp.concatenate([step[...]] * (start.shape[1] // 128), axis=1)
    out_iterate[...] = start[...] + wide * direction[...]
    out_residual[...] = residual[...] - wide * image[...]


def solution(mesh):
    n3 = mesh.shape["grp"]
    n2 = mesh.shape["sub"] // SEG

    def shards(
        right_side,
        iterate_in,
        diagonal,
        block_values,
        block_cols,
        couple_left,
        couple_right,
        send_rows,
        local_inverse,
        coarse_basis,
        coarse_diag,
        coarse_up,
    ):
        rows, cases = right_side.shape
        margin = send_rows.shape[2]
        whole = rows + 2 * margin
        modes = coarse_basis.shape[2]
        blocks, nonzeros, block = block_values.shape[1:4]
        members = n2 * SEG
        vmem = pltpu.VMEM
        dma = pltpu.SemaphoreType.DMA
        flat = vmem((cases, rows), F32)
        stay = pl.BlockSpec(memory_space=pl.ANY)
        step, direction, image, residual_start = pl.pallas_call(
            functools.partial(kernel, n2, n3),
            out_shape=[jax.ShapeDtypeStruct((cases, 128), F32)]
            + [jax.ShapeDtypeStruct((cases, rows), F32)] * 3,
            in_specs=[pl.BlockSpec(memory_space=pltpu.SMEM)] + [stay] * 11,
            out_specs=[pl.BlockSpec(memory_space=pltpu.VMEM)] + [stay] * 3,
            scratch_shapes=[
                flat,
                flat,
                vmem((blocks, 128), F32),
                vmem((1, rows), F32),
                vmem((blocks, nonzeros, block, block), BF16),
                vmem((rows, margin), BF16),
                vmem((rows, margin), BF16),
                vmem((whole, rows), BF16),
                vmem((2, margin), jnp.int32),
                vmem((whole, whole), BF16),
                vmem((modes, whole), BF16),
                vmem((modes, modes), F32),
                vmem((modes, modes), F32),
                vmem((2 * margin, rows), BF16),
                vmem((rows, 2 * margin), BF16),
                vmem((2, 2, cases, margin), BF16),
                vmem((2, 2, cases, margin), BF16),
                vmem((2, cases, 2 * margin), BF16),
                vmem((2, cases, 2 * margin), BF16),
                flat,
                vmem((cases, whole), BF16),
                vmem((cases, whole), F32),
                flat,
                vmem((SEG, 24, 128), F32),
                vmem((n2, 24, 128), F32),
                vmem((n3, 24, 128), F32),
                vmem((SEG, 8, 128), F32),
                vmem((SEG, 8, 128), F32),
                vmem((n2, 16, 128), F32),
                vmem((n3, 16, 128), F32),
                vmem((SEG, 8, 128), F32),
                vmem((SEG, 8, 128), F32),
                vmem((SEG, 32, 128), F32),
                vmem((n2, 32, 128), F32),
                vmem((n3, 32, 128), F32),
                vmem((64 + 8 * SLICE, 32 * SEG), F32),
                vmem((n2 + 1, 64 + 8 * SLICE, 32), F32),
                vmem((n3 + 1, 8 * SLICE, 32), F32),
                vmem((members, 4, 128), F32),
                vmem((n3, 4, 128), F32),
                dma((11,)),
                dma((3,)),
                dma((3, 2)),
                dma((3, 2)),
                dma((3, SEG)),
                dma((3, SEG)),
                dma((2, n2)),
                dma((2, n2)),
                dma((3, n3)),
                dma((3, n3)),
                dma((1, members)),
                dma((1, members)),
            ],
            compiler_params=pltpu.CompilerParams(
                collective_id=0, has_side_effects=True, vmem_limit_bytes=60 * 1024 * 1024
            ),
        )(
            block_cols.transpose(2, 0, 1),
            right_side.T,
            iterate_in.T,
            diagonal.reshape(blocks, 128),
            block_values,
            couple_left,
            couple_right,
            send_rows,
            local_inverse,
            coarse_basis[0].T,
            coarse_diag,
            coarse_up,
        )
        part = pl.BlockSpec((cases // PARTS, rows), lambda i: (i, 0))
        outs = pl.pallas_call(
            update,
            grid=(PARTS,),
            out_shape=[jax.ShapeDtypeStruct((cases, rows), F32)] * 2,
            in_specs=[pl.BlockSpec((cases // PARTS, 128), lambda i: (i, 0))] + [part] * 4,
            out_specs=[part] * 2,
        )(step, iterate_in.T, direction, residual_start, image)
        return tuple(out.T for out in outs)

    split = ("grp", "sub")
    in_specs = (
        P(split, None),
        P(split, None),
        P(split),
        P(split, None, None, None, None),
        P(split, None, None),
        P(split, None),
        P(split, None),
        P(split, None, None),
        P(split, None, None),
        P(split, None, None),
        P(split, None, None),
        P(split, None, None),
    )
    out_specs = (P(split, None), P(split, None))
    return jax.shard_map(
        shards, mesh=mesh, in_specs=in_specs, out_specs=out_specs, check_vma=False
    )
```

```python
import functools

import jax
import jax.numpy as jnp
from jax import lax
from jax.experimental import pallas as pl
from jax.experimental.pallas import tpu as pltpu
from jax.sharding import PartitionSpec as P

MESH = pl.DeviceIdType.MESH
HIGHEST = lax.Precision.HIGHEST
F32 = jnp.float32
BF16 = jnp.bfloat16
SEG = 8
PARTS = 2
SLICE = 3


def dot(a, b, ca=1, cb=0, precision=None):
    return lax.dot_general(
        a, b, (((ca,), (cb,)), ((), ())), precision=precision, preferred_element_type=F32
    )


def pack_block(x):
    return jnp.concatenate([x[8 * i : 8 * i + 8] for i in range(4)], axis=1)


def unpack_block(t):
    return jnp.concatenate([t[:, 32 * i : 32 * i + 32] for i in range(4)], axis=0)


def pack_slice(x):
    zeros = jnp.zeros((8, 32), F32)
    return jnp.concatenate([x[8 * i : 8 * i + 8] for i in range(SLICE)] + [zeros], axis=1)


def unpack_slice(t):
    return jnp.concatenate([t[:, 32 * i : 32 * i + 32] for i in range(SLICE)], axis=0)


def reduce_blocks(mats):
    sub = lax.broadcasted_iota(jnp.int32, (8, 128), 0)

    def wide(row):
        return jnp.broadcast_to(row, (8, 128))

    def four(state, q, p):
        g, kept, solved = state
        at = 8 * q + p
        later = range(q if p == 0 else q + 1, 4)
        cols = {
            i: [jnp.broadcast_to(g[i][:, at + j : at + j + 1], (8, 128)) for j in range(4)]
            for i in range(q, 4)
        }
        r0, r1, r2, r3 = [wide(g[q][p + j : p + j + 1, :]) for j in range(4)]

        def entry(i, j):
            return wide(cols[q][j][p + i : p + i + 1, :])

        a00, a01, a11 = entry(0, 0), entry(0, 1), entry(1, 1)
        a02, a03, a12, a13 = entry(0, 2), entry(0, 3), entry(1, 2), entry(1, 3)
        a22, a23, a33 = entry(2, 2), entry(2, 3), entry(3, 3)
        inv = 1.0 / (a00 * a11 - a01 * a01)
        i00, i01, i11 = a11 * inv, -a01 * inv, a00 * inv
        t02, t03 = i00 * a02 + i01 * a12, i00 * a03 + i01 * a13
        t12, t13 = i01 * a02 + i11 * a12, i01 * a03 + i11 * a13
        y0, y1 = i00 * r0 + i01 * r1, i01 * r0 + i11 * r1
        s22 = a22 - a02 * t02 - a12 * t12
        s23 = a23 - a02 * t03 - a12 * t13
        s33 = a33 - a03 * t03 - a13 * t13
        q2, q3 = r2 - a02 * y0 - a12 * y1, r3 - a03 * y0 - a13 * y1
        inv = 1.0 / (s22 * s33 - s23 * s23)
        w2 = (s33 * q2 - s23 * q3) * inv
        w3 = (s22 * q3 - s23 * q2) * inv
        w0 = y0 - t02 * w2 - t03 * w3
        w1 = y1 - t12 * w2 - t13 * w3
        w = (w0, w1, w2, w3)
        kept[q] = g[q] if p == 0 else jnp.where(sub < p, kept[q], g[q])
        for j in range(4):
            solved[q] = w0 if p + j == 0 else jnp.where(sub < p + j, solved[q], w[j])
        for i in later:
            c = cols[i]
            g[i] = g[i] - ((c[0] * w0 + c[1] * w1) + (c[2] * w2 + c[3] * w3))

    states = [([m[8 * i : 8 * i + 8] for i in range(4)], [None] * 4, [None] * 4) for m in mats]
    for q in range(4):
        for p in (0, 4):
            for state in states:
                four(state, q, p)
    return [
        dot(jnp.concatenate(kept, axis=0), jnp.concatenate(solved, axis=0), 0, 0, HIGHEST)
        for _, kept, solved in states
    ]


def levels_of(n):
    nodes = list(range(n))
    levels = []
    while len(nodes) > 1:
        ends = nodes + [n]
        levels.append([(ends[q], ends[q - 1], ends[q + 1]) for q in range(1, len(nodes), 2)])
        nodes = nodes[0::2]
    return levels


def identity_block():
    return (
        lax.broadcasted_iota(jnp.int32, (32, 32), 0) == lax.broadcasted_iota(jnp.int32, (32, 32), 1)
    ).astype(F32)


def products(inverse, augmented):
    return dot(augmented, dot(inverse, augmented, 1, 0, HIGHEST), 0, 0, HIGHEST)


def eliminate(n, diag, up, low, factors, loads=None, inverses=None, between=None):
    diag, up, low = list(diag), list(up), list(low)
    eye = identity_block()
    for depth, level in enumerate(levels_of(n)):
        known = inverses is not None and depth == 0
        first = jnp.zeros((32, 32), F32)
        augmented = [
            jnp.concatenate([first if known else diag[o], low[e], up[o], eye], axis=1)
            for o, e, _ in level
        ]
        if known:
            reduced = [products(inverses[o], m) for (o, _, _), m in zip(level, augmented)]
        else:
            reduced = reduce_blocks(augmented)
        for (o, e, f), full in zip(level, reduced):
            factors[o] = full[96:128]
            diag[e] = diag[e] - full[32:64, 32:64]
            diag[f] = diag[f] - full[64:96, 64:96]
            up[e] = -full[32:64, 64:96]
            low[e] = -full[64:96, 32:64]
            if loads is not None:
                moved = dot(loads[o], full[96:128], 1, 0, HIGHEST)
                loads[e] = loads[e] - moved[:, 32:64]
                loads[f] = loads[f] - moved[:, 64:96]
        if between is not None and depth == 1:
            between()
    return diag[0], up[0], low[0], diag[n]


def sweep_up(n, loads, factors):
    loads = list(loads)
    for level in levels_of(n):
        for o, e, f in level:
            moved = dot(loads[o], factors[o], 1, 0, HIGHEST)
            loads[e] = loads[e] - moved[:, 32:64]
            loads[f] = loads[f] - moved[:, 64:96]
    return loads


def sweep_down(n, loads, first, last, factors):
    sol = [None] * (n + 1)
    sol[0], sol[n] = first, last
    blank = jnp.zeros_like(first)
    for level in reversed(levels_of(n)):
        for o, e, f in level:
            known = jnp.concatenate([blank, -sol[e], -sol[f], loads[o]], axis=1)
            sol[o] = dot(known, factors[o], 1, 1, HIGHEST)
    return sol


def response(n, loads, factors):
    eye, rows = identity_block(), loads[0].shape[0]
    none, short = jnp.zeros((32, 32), F32), jnp.zeros((rows, 32), F32)
    first = jnp.concatenate([eye, none, short], axis=0)
    last = jnp.concatenate([none, eye, short], axis=0)
    padded = [jnp.concatenate([none, none, x], axis=0) for x in loads]
    return sweep_down(n, padded, first, last, factors)


def kernel(
    n2,
    n3,
    cols_ref,
    rhs_hbm,
    start_hbm,
    diag_hbm,
    values_hbm,
    left_hbm,
    right_hbm,
    rows_hbm,
    inverse_hbm,
    basis_hbm,
    cdiag_hbm,
    cup_hbm,
    out_step,
    out_direction,
    out_image,
    out_start,
    rhs,
    start,
    diag_rows,
    diag,
    values,
    couple_left,
    couple_right,
    weights,
    rows_v,
    inverse,
    basis,
    cdiag,
    cup,
    pick,
    spread,
    halo_out,
    halo_in,
    edge_out,
    edge_in,
    residual,
    extended,
    correction,
    image,
    m1,
    m2,
    m3,
    s1_out,
    s1,
    s2,
    s3,
    s4_out,
    s4,
    f1,
    f2,
    f3,
    reply,
    x2,
    x3,
    r1,
    r2,
    load_sem,
    store_sem,
    ring_send,
    ring_recv,
    seg_send,
    seg_recv,
    mid_send,
    mid_recv,
    top_send,
    top_recv,
    sub_send,
    sub_recv,
):
    cases, rows_own = start.shape
    margin = rows_v.shape[1]
    row_blocks = rows_own // 128
    own = slice(margin, margin + rows_own)
    after = slice(margin + rows_own, 2 * margin + rows_own)
    grp, sub = lax.axis_index("grp"), lax.axis_index("sub")
    members = n2 * SEG
    pos1, pos2 = lax.rem(sub, SEG), lax.div(sub, SEG)
    rank = grp * members + sub
    total = n3 * members
    sub_next, sub_prev = lax.rem(sub + 1, members), lax.rem(sub + members - 1, members)
    grp_next = lax.rem(grp + (sub + 1) // members, n3)
    grp_prev = lax.rem(grp + n3 - (members - sub) // members, n3)
    ring = [(grp_prev, sub_prev), (grp_next, sub_next)]
    has_prev, has_next = rank > 0, rank < total - 1

    def seg_other(off):
        j = lax.rem(pos1 + off, SEG)
        return j, (grp, pos2 * SEG + j)

    def mid_other(off):
        j = lax.rem(pos2 + off, n2)
        return j, (grp, j * SEG + pos1)

    def top_other(off):
        j = lax.rem(grp + off, n3)
        return j, (j, sub)

    def sub_other(off):
        j = lax.rem(sub + off, members)
        return j, (grp, j)

    kinds = {
        "seg": (SEG, pos1, seg_other, seg_send, seg_recv),
        "mid": (n2, pos2, mid_other, mid_send, mid_recv),
        "top": (n3, grp, top_other, top_send, top_recv),
        "sub": (members, sub, sub_other, sub_send, sub_recv),
    }

    loads = {}
    for name, source, target in (
        ("rows", rows_hbm.at[0], rows_v),
        ("start", start_hbm, start),
        ("cdiag", cdiag_hbm.at[0], cdiag),
        ("cup", cup_hbm.at[0], cup),
        ("values", values_hbm.at[0], values),
        ("left", left_hbm, couple_left),
        ("right", right_hbm, couple_right),
        ("diag", diag_hbm, diag_rows),
        ("rhs", rhs_hbm, rhs),
        ("basis", basis_hbm, basis),
        ("inverse", inverse_hbm.at[0], inverse),
    ):
        copy = pltpu.make_async_copy(source, target, load_sem.at[len(loads)])
        copy.start()
        loads[name] = copy

    barrier = pltpu.get_barrier_semaphore()
    greeted = 0
    for kind in ("sub", "top"):
        n, _, other, _, _ = kinds[kind]
        for off in sorted(range(1, n), key=lambda o: -min(o, n - o)):
            pl.semaphore_signal(barrier, inc=1, device_id=other(off)[1], device_id_type=MESH)
            greeted += 1
    for target in ring:
        pl.semaphore_signal(barrier, inc=1, device_id=target, device_id_type=MESH)
        greeted += 1

    sends = []

    def ring_exchange(step, outgoing, incoming):
        for side in range(2):
            copy = pltpu.make_async_remote_copy(
                src_ref=outgoing.at[side],
                dst_ref=incoming.at[1 - side],
                send_sem=ring_send.at[step, side],
                recv_sem=ring_recv.at[step, 1 - side],
                device_id=ring[side],
                device_id_type=MESH,
            )
            copy.start()
            sends.append(copy)

        def wait():
            for side in range(2):
                pltpu.make_async_remote_copy(
                    src_ref=outgoing.at[1 - side],
                    dst_ref=incoming.at[side],
                    send_sem=ring_send.at[step, 1 - side],
                    recv_sem=ring_recv.at[step, side],
                    device_id=ring[side],
                    device_id_type=MESH,
                ).wait_recv()

        return wait

    def all_to_all(kind, step, outgoing, incoming):
        n, place, other, send, recv = kinds[kind]
        order = sorted(range(1, n), key=lambda o: -min(o, n - o))
        for off in order:
            j, target = other(off)
            copy = pltpu.make_async_remote_copy(
                src_ref=incoming.at[place] if outgoing is None else outgoing.at[j],
                dst_ref=incoming.at[place],
                send_sem=send.at[step, off],
                recv_sem=recv.at[step, off],
                device_id=target,
                device_id_type=MESH,
            )
            copy.start()
            sends.append(copy)

        def wait():
            for off in reversed(order):
                source, target = other(n - off)
                pltpu.make_async_remote_copy(
                    src_ref=incoming.at[source],
                    dst_ref=incoming.at[source],
                    send_sem=send.at[step, off],
                    recv_sem=recv.at[step, off],
                    device_id=target,
                    device_id_type=MESH,
                ).wait_recv()

        return wait

    loads["rows"].wait()
    for side in range(2):
        here = slice(side * margin, (side + 1) * margin)
        row = lax.broadcasted_iota(jnp.int32, (rows_own, margin), 0)
        listed = rows_v[side : side + 1, :]
        spread[:, here] = (row == jnp.broadcast_to(listed, (rows_own, margin))).astype(F32).astype(BF16)

    def picked(source):
        return dot(source, spread[...]).astype(BF16)

    loads["start"].wait()
    extended[:, own] = start[...].astype(BF16)
    loads["cdiag"].wait()
    loads["cup"].wait()
    blank = jnp.zeros((32, 32), F32)
    augmented = jnp.concatenate([cdiag[...], blank, blank, identity_block()], axis=1)
    m1[pos1, 16:24] = pack_block(reduce_blocks([augmented])[0][96:128, 96:128])
    m1[pos1, 0:8] = pack_block(cdiag[...])
    m1[pos1, 8:16] = pack_block(jnp.where(has_next, cup[...], 0.0))
    chosen = picked(extended[:, own])
    halo_out[0, 0] = chosen[:, :margin]
    halo_out[0, 1] = chosen[:, margin:]

    pl.semaphore_wait(barrier, greeted)
    wait_m1 = all_to_all("seg", 0, None, m1)
    wait_h1 = ring_exchange(0, halo_out.at[0], halo_in.at[0])

    loads["values"].wait()
    for i in range(row_blocks):
        turned = [values[i, t].T for t in range(values.shape[1])]
        for c in range(row_blocks):
            block = None
            for t, term in enumerate(turned):
                here = (jnp.full((1, 128), cols_ref[t, 0, i], jnp.int32) == c).astype(F32).astype(BF16)
                block = term * here if block is None else block + term * here
            weights[margin + 128 * c : margin + 128 * (c + 1), 128 * i : 128 * (i + 1)] = block
    loads["left"].wait()
    loads["right"].wait()
    for i in range(row_blocks):
        here = slice(128 * i, 128 * (i + 1))
        weights[0:margin, here] = couple_left[here, :].T
        weights[after, here] = couple_right[here, :].T
    loads["diag"].wait()
    for i in range(row_blocks):
        diag[:, 128 * i : 128 * (i + 1)] = diag_rows[i : i + 1, :]
    loads["rhs"].wait()
    residual[...] = rhs[...] - (diag[...] * start[...] + dot(extended[:, own], weights[own, :]))
    wait_h1()
    nothing = jnp.zeros((cases, margin), BF16)
    from_left = jnp.where(has_prev, halo_in[0, 0], nothing)
    from_right = jnp.where(has_next, halo_in[0, 1], nothing)
    residual[...] = residual[...] - (
        dot(from_left, weights[0:margin, :]) + dot(from_right, weights[after, :])
    )
    extended[:, own] = residual[...].astype(BF16)
    chosen = picked(extended[:, own])
    halo_out[1, 0] = chosen[:, :margin]
    halo_out[1, 1] = chosen[:, margin:]
    wait_h2 = ring_exchange(1, halo_out.at[1], halo_in.at[1])

    first_group = [(j * (cases // 8)) // SEG for j in range(SEG)]
    pending = []

    def start_coarse():
        wait_h2()
        extended[:, 0:margin] = jnp.where(has_prev, halo_in[1, 0], nothing)
        extended[:, after] = jnp.where(has_next, halo_in[1, 1], nothing)
        loads["basis"].wait()
        coarse_in = dot(extended[...], basis[...], 1, 1)
        for j in range(SEG):
            at = 8 * first_group[j]
            s1_out[j] = pack_slice(coarse_in[at : at + 8 * SLICE])
        s1[pos1] = s1_out[pos1]
        pending.append(all_to_all("seg", 1, s1_out, s1))

    wait_m1()
    cdiags = [unpack_block(m1[i, 0:8]) for i in range(SEG)] + [jnp.zeros((32, 32), F32)]
    ups = [unpack_block(m1[i, 8:16]) for i in range(SEG)]
    inverses = [unpack_block(m1[i, 16:24]) for i in range(SEG)]
    d0, u0, _, dn = eliminate(SEG, cdiags, ups, [u.T for u in ups], f1, None, inverses, start_coarse)
    m2[pos2, 0:8] = pack_block(d0)
    m2[pos2, 8:16] = pack_block(u0)
    m2[pos2, 16:24] = pack_block(dn)
    wait_m2 = all_to_all("mid", 0, None, m2)

    for side in range(2):
        standing = jnp.broadcast_to(rows_v[side : side + 1, :], (margin, margin)).astype(F32).T
        for c in range(row_blocks):
            place = (lax.broadcasted_iota(jnp.int32, (margin, 128), 1) + 128 * c).astype(F32)
            pick[side * margin : (side + 1) * margin, 128 * c : 128 * (c + 1)] = (
                standing == place
            ).astype(F32).astype(BF16)

    loads["inverse"].wait()
    for c in range(0, correction.shape[1], 256):
        correction[:, c : c + 256] = dot(extended[...], inverse[:, c : c + 256])

    def gathered(n, messages):
        blocks = [[unpack_block(messages[i, 8 * q : 8 * q + 8]) for q in range(3)] for i in range(n)]
        summed = [blocks[0][0]]
        for i in range(1, n):
            summed.append(blocks[i][0] + blocks[i - 1][2])
        return summed + [blocks[n - 1][2]], [b[1] for b in blocks], [b[1].T for b in blocks]

    def gathered_loads(n, messages):
        a = [unpack_slice(messages[i, 0:8]) for i in range(n)]
        b = [unpack_slice(messages[i, 8:16]) for i in range(n)]
        return [a[0]] + [a[i] + b[i - 1] for i in range(1, n)] + [b[n - 1]]

    pending[0]()
    loads1 = [unpack_slice(s1[i]) for i in range(SEG)] + [jnp.zeros((8 * SLICE, 32), F32)]
    loads1 = sweep_up(SEG, loads1, f1)
    s2[pos2, 0:8] = pack_slice(loads1[0])
    s2[pos2, 8:16] = pack_slice(loads1[SEG])
    wait_s2 = all_to_all("mid", 1, None, s2)
    reply1 = response(SEG, loads1, f1)
    for i in range(SEG):
        reply[:, 32 * i : 32 * i + 32] = reply1[i]

    wait_m2()
    d0, u0, _, dn = eliminate(n2, *gathered(n2, m2), f2)
    m3[grp, 0:8] = pack_block(d0)
    m3[grp, 8:16] = pack_block(u0)
    m3[grp, 16:24] = pack_block(dn)
    wait_m3 = all_to_all("top", 0, None, m3)
    wait_s2()
    loads2 = sweep_up(n2, gathered_loads(n2, s2), f2)
    s3[grp, 0:8] = pack_slice(loads2[0])
    s3[grp, 8:16] = pack_slice(loads2[n2])
    wait_s3 = all_to_all("top", 1, None, s3)
    reply2 = response(n2, loads2, f2)
    for i in range(n2 + 1):
        x2[i] = reply2[i]
    ends = jnp.concatenate([x2[pos2], x2[pos2 + 1]], axis=1)
    through = dot(ends, reply[0:64], 1, 0, HIGHEST)
    reply[0:64] = through[0:64]
    reply[64:] = through[64:] + reply[64:]

    wait_m3()
    wait_s3()
    loads3 = gathered_loads(n3, s3)
    d0, u0, _, _ = eliminate(n3, *gathered(n3, m3), f3, loads3)
    augmented = jnp.concatenate([d0, blank, blank, identity_block()], axis=1)
    f3[0] = reduce_blocks([augmented])[0][96:128]
    none = jnp.zeros((8 * SLICE, 32), F32)
    first = dot(jnp.concatenate([none, none, none, loads3[0]], axis=1), f3[0], 1, 1, HIGHEST)
    sol3 = sweep_down(n3, loads3, first, none, f3)
    for i in range(n3 + 1):
        x3[i] = sol3[i]
    ends = jnp.concatenate([x3[grp], x3[grp + 1]], axis=1)
    sol1 = dot(ends, reply[0:64], 1, 0, HIGHEST) + reply[64:]
    for j in range(SEG):
        s4_out[j] = pack_slice(sol1[:, 32 * j : 32 * j + 32])
    s4[pos1] = s4_out[pos1]
    wait_s4 = all_to_all("seg", 2, s4_out, s4)
    wait_s4()
    pieces = []
    for group in range(cases // 8):
        j = [j for j in range(SEG) if first_group[j] <= group < first_group[j] + SLICE][0]
        q = group - first_group[j]
        pieces.append(s4[j][:, 32 * q : 32 * q + 32])
    coarse_sol = jnp.concatenate(pieces, axis=0).astype(BF16)

    correction[...] = correction[...] + dot(coarse_sol, basis[...])
    chosen = picked(correction[:, own].astype(BF16))
    edge_out[0, :, 0:margin] = correction[:, 0:margin].astype(BF16)
    edge_out[1, :, 0:margin] = correction[:, after].astype(BF16)
    edge_out[0, :, margin:] = chosen[:, :margin]
    edge_out[1, :, margin:] = chosen[:, margin:]
    wait_edge = ring_exchange(2, edge_out, edge_in)
    wait_edge()
    extended[:, 0:margin] = jnp.where(has_prev, edge_in[0, :, 0:margin], nothing)
    extended[:, margin : 2 * margin] = jnp.where(has_next, edge_in[1, :, 0:margin], nothing)
    owned = correction[:, own] + dot(extended[:, 0 : 2 * margin], pick[...])
    before = (edge_in[0, :, margin:].astype(F32) + correction[:, 0:margin]).astype(BF16)
    beyond = (edge_in[1, :, margin:].astype(F32) + correction[:, after]).astype(BF16)
    correction[:, own] = owned
    extended[:, own] = owned.astype(BF16)
    extended[:, 0:margin] = jnp.where(has_prev, before, nothing)
    extended[:, after] = jnp.where(has_next, beyond, nothing)
    image[...] = diag[...] * correction[:, own] + dot(extended[...], weights[...])
    stores = []
    for source, target in (
        (correction.at[:, own], out_direction),
        (image, out_image),
        (residual, out_start),
    ):
        stores.append(pltpu.make_async_copy(source, target, store_sem.at[len(stores)]))
        stores[-1].start()

    def column_sums(x):
        total = x[:, 0:128]
        for i in range(1, row_blocks):
            total = total + x[:, 128 * i : 128 * (i + 1)]
        row = jnp.sum(total.T, axis=0, keepdims=True)
        rest = jnp.concatenate([row[:, 128:cases], jnp.zeros((1, 256 - cases), F32)], axis=1)
        return [row[:, 0:128], rest]

    inner = column_sums(residual[...] * correction[:, own])
    curvature = column_sums(correction[:, own] * image[...])
    part = jnp.concatenate(inner + curvature, axis=0)
    for kind, buffer, step in (("sub", r1, 0), ("top", r2, 2)):
        n, place = kinds[kind][:2]
        buffer[place] = part
        all_to_all(kind, step, None, buffer)()
        part = buffer[0]
        for i in range(1, n):
            part = part + buffer[i]
    ratio = part[0:2] / part[2:4]
    step_row = jnp.concatenate([ratio[0:1, :], ratio[1:2, : cases - 128]], axis=1)
    out_step[...] = jnp.broadcast_to(step_row, (128, cases)).T
    for copy in stores:
        copy.wait()
    for copy in sends:
        copy.wait_send()


def update(step, start, direction, residual, image, out_iterate, out_residual):
    wide = jnp.concatenate([step[...]] * (start.shape[1] // 128), axis=1)
    out_iterate[...] = start[...] + wide * direction[...]
    out_residual[...] = residual[...] - wide * image[...]


def solution(mesh):
    n3 = mesh.shape["grp"]
    n2 = mesh.shape["sub"] // SEG

    def shards(
        right_side,
        iterate_in,
        diagonal,
        block_values,
        block_cols,
        couple_left,
        couple_right,
        send_rows,
        local_inverse,
        coarse_basis,
        coarse_diag,
        coarse_up,
    ):
        rows, cases = right_side.shape
        margin = send_rows.shape[2]
        whole = rows + 2 * margin
        modes = coarse_basis.shape[2]
        blocks, nonzeros, block = block_values.shape[1:4]
        members = n2 * SEG
        vmem = pltpu.VMEM
        dma = pltpu.SemaphoreType.DMA
        flat = vmem((cases, rows), F32)
        stay = pl.BlockSpec(memory_space=pl.ANY)
        step, direction, image, residual_start = pl.pallas_call(
            functools.partial(kernel, n2, n3),
            out_shape=[jax.ShapeDtypeStruct((cases, 128), F32)]
            + [jax.ShapeDtypeStruct((cases, rows), F32)] * 3,
            in_specs=[pl.BlockSpec(memory_space=pltpu.SMEM)] + [stay] * 11,
            out_specs=[pl.BlockSpec(memory_space=pltpu.VMEM)] + [stay] * 3,
            scratch_shapes=[
                flat,
                flat,
                vmem((blocks, 128), F32),
                vmem((1, rows), F32),
                vmem((blocks, nonzeros, block, block), BF16),
                vmem((rows, margin), BF16),
                vmem((rows, margin), BF16),
                vmem((whole, rows), BF16),
                vmem((2, margin), jnp.int32),
                vmem((whole, whole), BF16),
                vmem((modes, whole), BF16),
                vmem((modes, modes), F32),
                vmem((modes, modes), F32),
                vmem((2 * margin, rows), BF16),
                vmem((rows, 2 * margin), BF16),
                vmem((2, 2, cases, margin), BF16),
                vmem((2, 2, cases, margin), BF16),
                vmem((2, cases, 2 * margin), BF16),
                vmem((2, cases, 2 * margin), BF16),
                flat,
                vmem((cases, whole), BF16),
                vmem((cases, whole), F32),
                flat,
                vmem((SEG, 24, 128), F32),
                vmem((n2, 24, 128), F32),
                vmem((n3, 24, 128), F32),
                vmem((SEG, 8, 128), F32),
                vmem((SEG, 8, 128), F32),
                vmem((n2, 16, 128), F32),
                vmem((n3, 16, 128), F32),
                vmem((SEG, 8, 128), F32),
                vmem((SEG, 8, 128), F32),
                vmem((SEG, 32, 128), F32),
                vmem((n2, 32, 128), F32),
                vmem((n3, 32, 128), F32),
                vmem((64 + 8 * SLICE, 32 * SEG), F32),
                vmem((n2 + 1, 64 + 8 * SLICE, 32), F32),
                vmem((n3 + 1, 8 * SLICE, 32), F32),
                vmem((members, 4, 128), F32),
                vmem((n3, 4, 128), F32),
                dma((11,)),
                dma((3,)),
                dma((3, 2)),
                dma((3, 2)),
                dma((3, SEG)),
                dma((3, SEG)),
                dma((2, n2)),
                dma((2, n2)),
                dma((3, n3)),
                dma((3, n3)),
                dma((1, members)),
                dma((1, members)),
            ],
            compiler_params=pltpu.CompilerParams(
                collective_id=0, has_side_effects=True, vmem_limit_bytes=60 * 1024 * 1024
            ),
        )(
            block_cols.transpose(2, 0, 1),
            right_side.T,
            iterate_in.T,
            diagonal.reshape(blocks, 128),
            block_values,
            couple_left,
            couple_right,
            send_rows,
            local_inverse,
            coarse_basis[0].T,
            coarse_diag,
            coarse_up,
        )
        part = pl.BlockSpec((cases // PARTS, rows), lambda i: (i, 0))
        outs = pl.pallas_call(
            update,
            grid=(PARTS,),
            out_shape=[jax.ShapeDtypeStruct((cases, rows), F32)] * 2,
            in_specs=[pl.BlockSpec((cases // PARTS, 128), lambda i: (i, 0))] + [part] * 4,
            out_specs=[part] * 2,
        )(step, iterate_in.T, direction, residual_start, image)
        return tuple(out.T for out in outs)

    split = ("grp", "sub")
    in_specs = (
        P(split, None),
        P(split, None),
        P(split),
        P(split, None, None, None, None),
        P(split, None, None),
        P(split, None),
        P(split, None),
        P(split, None, None),
        P(split, None, None),
        P(split, None, None),
        P(split, None, None),
        P(split, None, None),
    )
    out_specs = (P(split, None), P(split, None))
    return jax.shard_map(
        shards, mesh=mesh, in_specs=in_specs, out_specs=out_specs, check_vma=False
    )
```
